32 devices in a mesh: pipe: 4 (over z), dp: 8 (over y, x, core).
Axes of the slice: x: 2, y: 2, z: 4, core: 2. Of those that a mesh axis runs over, the one named last changes fastest.
Arguments:
- acts: bfloat16 [4, 1024, 5120], P('pipe', 'dp'), may hold values from -6 to 6
- cotangent: bfloat16 [1024, 5120], P('dp'), may hold values from -0.59765625 to 0.59765625
- kv_grads: bfloat16 [4, 1024, 2048], P('pipe', 'dp'), may hold values from -6 to 6
- w_kv: bfloat16 [4, 5120, 2048], P('pipe'), may hold values from -0.0078125 to 0.0078125
- momentum: bfloat16 [4, 5120, 2048], P('pipe', 'dp'), may hold values from -0.119628906 to 0.119628906
Outputs:
- update: bfloat16 [4, 5120, 2048], P('pipe', 'dp')
- input_grads: bfloat16 [4, 1024, 5120], P('pipe', 'dp')
The draws below stay inside these ranges and needn't reach their ends.
All inputs are finite; a program needn't handle non-finite values.
Results may differ from the reference program's by a relative error of at most 0.022.
Values may be sent and summed in bfloat16 or wider, within the bound.
No kernel may reach another device: no remote copies, remote signals or barrier semaphores. Data moves between devices by JAX's collectives and lax.ppermute only.
A program may use at most 128 MiB of HBM per device.

```python
import math
import jax
import jax.numpy as jnp
from jax import lax

D = 5120
HEAD = 128
TOK_DEV = 128
ITERS = 5
LAT = 1024
MATS = 16
SECTIONS = 4
TOKENS = 1024
N_DP = 8


def raised(entries, own_key, source, target, parts, factor):
    def block_of(dim):
        return (jnp.arange(entries.shape[dim]) // (entries.shape[dim] // parts)).reshape((-1,) + (1,) * (entries.ndim - 1 - dim))

    first = jax.random.permutation(own_key, parts)[block_of(target)]
    other_side = (block_of(target) + parts // 2) % parts
    return jnp.where((block_of(source) == first) | (block_of(source) == other_side), factor * entries, entries)


def steps_of(key, dims, shards, least, top_value):
    factor_of, own = 1.0, jax.random.fold_in(key, 6)
    for axis_at, parts in shards:
        steps = jnp.exp(jax.random.uniform(jax.random.fold_in(own, axis_at), (parts,), jnp.float32, least / len(shards), top_value / len(shards)))
        factor_of = factor_of * jnp.repeat(steps, dims[axis_at] // parts).reshape([-1 if axis == axis_at else 1 for axis in range(len(dims))])
    return factor_of


def gaussian(rng, dims, width, reach, shards=(), held_as=jnp.bfloat16):
    factor_of = steps_of(rng, dims, shards, -0.22, 0.18) if shards else 1.0
    array = jax.random.normal(rng, dims, jnp.float32) * width * factor_of
    return jnp.minimum(jnp.maximum(array, -reach), reach).astype(held_as)


def bell_draw_with(own_key, dims, scale, limit, cuts, heavy, kind=jnp.bfloat16):
    array = scale * jax.random.normal(own_key, dims, jnp.float32)
    if cuts:
        array = array * steps_of(own_key, dims, cuts, -0.22, 0.18)
    return jnp.clip(raised(array, jax.random.fold_in(own_key, 3), *heavy), -limit, limit).astype(kind)


def setup_inputs(seed: int = 0) -> dict:
    arg_keys = jax.random.split(jax.random.key(seed), 6)
    return {
        "acts": bell_draw_with(arg_keys[0], (SECTIONS, TOKENS, D), 1.0, 6.0, ((0, 4), (1, 8)), (1, 2, 8, 2.0)),
        "cotangent": gaussian(arg_keys[1], (TOKENS, D), 0.1, 0.59765625, ((0, 8),)),
        "kv_grads": gaussian(arg_keys[2], (SECTIONS, TOKENS, 2 * LAT), 1.0, 6.0, ((0, 4), (1, 8))),
        "w_kv": gaussian(arg_keys[3], (SECTIONS, D, 2 * LAT), (100 * D) ** -0.5, 0.0078125, ((0, 4),)),
        "momentum": gaussian(arg_keys[4], (SECTIONS, D, 2 * LAT), 0.02, 0.119628906, ((0, 4), (1, 8))),
    }


momentum_rate = 0.95
quintic_a = 3.4445
quintic_b = -4.775
quintic_c = 2.0315
epsilon = 1e-07

def layer_back(incoming, kv_rows, weights):
    return (incoming.astype(jnp.float32) + jnp.dot(kv_rows, weights.T, preferred_element_type=jnp.float32)).astype(jnp.bfloat16)

def partial_sums(inputs, kv_rows):

    def shaped(values):
        return values.reshape(N_DP, TOK_DEV, values.shape[1])

    def accumulate(total, pieces):
        rows_in, rows_kv = pieces
        term = jnp.dot(rows_in.T, rows_kv, preferred_element_type=jnp.float32) * (1.0 / TOKENS)
        rounded = lax.optimization_barrier(term.astype(jnp.bfloat16))
        return (total + rounded.astype(jnp.float32), None)
    start = jnp.zeros((D, 2 * LAT), jnp.float32)
    total, unused = lax.scan(accumulate, start, (shaped(inputs), shaped(kv_rows)))
    return total

def orthogonalize(buffer):
    values = buffer.astype(jnp.float32)
    squares = lax.optimization_barrier(jnp.sum(values * values, axis=(1, 2), keepdims=True))
    current = values / (jnp.sqrt(squares) + epsilon)
    highest = lax.Precision.HIGHEST
    for step in range(ITERS):
        gram = jnp.einsum('mri,mrj->mij', current, current, precision=highest)
        mixer = quintic_b * gram + quintic_c * jnp.einsum('mij,mjk->mik', gram, gram, precision=highest)
        current = quintic_a * current + jnp.einsum('mri,mij->mrj', current, mixer, precision=highest)
    return current

def reference(acts, cotangent, kv_grads, w_kv, momentum):
    scale = 0.2 * math.sqrt(max(D, HEAD))
    incoming = cotangent
    updates = [None] * SECTIONS
    grads = [None] * SECTIONS
    for section in reversed(range(SECTIONS)):
        outgoing = layer_back(incoming, kv_grads[section], w_kv[section])
        grad = partial_sums(acts[section], kv_grads[section])
        buffer = (momentum_rate * momentum[section].astype(jnp.float32) + grad).astype(jnp.bfloat16)
        matrices = buffer.reshape(D, MATS, HEAD).transpose(1, 0, 2)
        result = orthogonalize(matrices)
        final = (scale * result).astype(jnp.bfloat16)
        updates[section] = final.transpose(1, 0, 2).reshape(D, MATS * HEAD)
        grads[section] = outgoing
        incoming = outgoing
    return (jnp.stack(updates), jnp.stack(grads))
```

```python
import functools
import math

import jax
import jax.numpy as jnp
from jax import lax
from jax.experimental import pallas as pl
from jax.experimental.pallas import tpu as pltpu
from jax.sharding import PartitionSpec as P

HEAD = 128
ITERS = 5
CORES = 2
CHUNKS = 4
LAG = 2

momentum_rate = 0.95
quintic_a = 3.4445
quintic_b = -4.775
quintic_c = 2.0315
epsilon = 1e-07

VMEM_LIMIT = 48 * 1024 * 1024
F32 = jnp.float32
BF16 = jnp.bfloat16


def cost(flops, moved):
    return pl.CostEstimate(flops=int(flops), bytes_accessed=int(moved), transcendentals=0)


def whole():
    return pl.BlockSpec(memory_space=pltpu.VMEM)


def params():
    return pltpu.CompilerParams(vmem_limit_bytes=VMEM_LIMIT)


def swap(value, by):
    count = lax.axis_size("dp")
    return lax.ppermute(value, "dp", [(i, i ^ by) for i in range(count)])


def down(value):
    count = lax.axis_size("pipe")
    return lax.ppermute(value, "pipe", [(i, i - 1) for i in range(1, count)])


def gather_tokens(rows):
    count = lax.axis_size("dp")
    chips = count // CORES
    held = {0: [rows]}
    if chips == 4:
        half = rows.shape[0] // 2
        first, second = swap(rows, CORES), swap(rows, 2 * CORES)
        held[1], held[2] = [first], [second]
        held[3] = [swap(first[:half], 2 * CORES), swap(second[half:], CORES)]
    else:
        for distance in range(1, chips):
            held[distance] = [swap(rows, CORES * distance)]
    result = []
    for distance in range(chips):
        result.append((CORES * distance, held[distance]))
    for distance in range(chips):
        result.append((CORES * distance + 1, [swap(v, 1) for v in held[distance]]))
    return result


def split_columns(inputs):
    count = lax.axis_size("dp")
    tokens, width = inputs.shape
    block = width // count

    def kernel(in_ref, *out_refs):
        own = lax.axis_index("dp")
        for distance in range(count):
            owner = own ^ distance
            columns = pl.ds(pl.multiple_of(owner * block, 128), block) if block % 128 == 0 else None
            if columns is None:
                for other in range(count):
                    @pl.when(owner == other)
                    def store():
                        piece = in_ref[:, other * block : (other + 1) * block]
                        out_refs[distance // CORES][distance % CORES] = piece.T
            else:
                out_refs[distance // CORES][distance % CORES] = in_ref[:, columns].T

    shape = jax.ShapeDtypeStruct((CORES, block, tokens), BF16)
    return pl.pallas_call(
        kernel,
        out_shape=[shape] * (count // CORES),
        in_specs=[whole()],
        out_specs=[whole()] * (count // CORES),
        compiler_params=params(),
        cost_estimate=cost(0, 4 * tokens * width),
        name="split_columns",
    )(inputs)


def gradient(parts, moment, scale, slots):
    rows, width = moment.shape
    count = lax.axis_size("dp")
    chips = count // CORES
    mats = width // HEAD
    per_step = 2 if mats % 2 == 0 else 1
    block = per_step * HEAD
    left = [a for a, pieces in parts]
    right = [piece for a, pieces in parts for piece in pieces]
    tokens = sum(piece.shape[0] for piece in right)
    n_left, n_right = len(left), len(right)

    def kernel(*refs):
        left_refs = refs[:n_left]
        right_refs = refs[n_left : n_left + n_right]
        mom_ref, buf_ref, mine_ref, theirs_ref, held = refs[n_left + n_right :]
        step = pl.program_id(0)
        own = lax.axis_index("dp")

        @pl.when(step == 0)
        def load():
            at = 0
            for ref in left_refs:
                held[:, at : at + ref.shape[1]] = ref[...]
                at += ref.shape[1]
            mine_ref[...] = jnp.zeros_like(mine_ref)
            theirs_ref[...] = jnp.zeros_like(theirs_ref)

        kv_block = jnp.concatenate([ref[...] for ref in right_refs], axis=0)
        grad = jnp.dot(held[...], kv_block, preferred_element_type=F32)
        buffer = (momentum_rate * mom_ref[...].astype(F32) + grad * scale).astype(BF16)
        buf_ref[...] = buffer
        gram = lax.dot_general(buffer, buffer, (((0,), (0,)), ((), ())), preferred_element_type=F32)
        for which in range(per_step):
            span = slice(which * HEAD, (which + 1) * HEAD)
            mat = step * per_step + which
            place = mat // slots
            core = place // chips
            apart = (place % chips) ^ (own // CORES)

            @pl.when(core == own % CORES)
            def keep():
                mine_ref[apart, mat % slots] = gram[span, span]

            @pl.when(core != own % CORES)
            def give():
                theirs_ref[apart, mat % slots] = gram[span, span]

    gram_shape = jax.ShapeDtypeStruct((chips, slots, HEAD, HEAD), F32)
    gram_spec = pl.BlockSpec((chips, slots, HEAD, HEAD), lambda j: (0, 0, 0, 0))
    column = lambda height: pl.BlockSpec((height, block), lambda j: (0, j))
    return pl.pallas_call(
        kernel,
        grid=(mats // per_step,),
        out_shape=[jax.ShapeDtypeStruct((rows, width), BF16), gram_shape, gram_shape],
        in_specs=[pl.BlockSpec(a.shape, lambda j: (0, 0)) for a in left]
        + [column(piece.shape[0]) for piece in right]
        + [column(rows)],
        out_specs=[column(rows), gram_spec, gram_spec],
        scratch_shapes=[pltpu.VMEM((rows, tokens), BF16)],
        compiler_params=params(),
        cost_estimate=cost(2 * rows * tokens * width, 2 * tokens * (rows + width) + 4 * rows * width),
        name="gradient",
    )(*left, *right, moment)


def add_pairs(first, second):
    chips = first.shape[0]

    def kernel(first_ref, second_ref, *out_refs):
        for distance in range(chips):
            out_refs[distance][...] = first_ref[distance] + second_ref[distance]

    shape = jax.ShapeDtypeStruct(first.shape[1:], F32)
    return pl.pallas_call(
        kernel,
        out_shape=[shape] * chips,
        in_specs=[whole()] * 2,
        out_specs=[whole()] * chips,
        compiler_params=params(),
        name="add_pairs",
    )(first, second)


def mixing(grams, scale):
    slots = grams[0].shape[0]
    highest = lax.Precision.HIGHEST

    def product(left, right):
        return jnp.dot(left, right, precision=highest, preferred_element_type=F32)

    def kernel(*refs):
        gram_refs, out_ref = refs[:-1], refs[-1]
        row = lax.broadcasted_iota(jnp.int32, (HEAD, HEAD), 0)
        col = lax.broadcasted_iota(jnp.int32, (HEAD, HEAD), 1)
        eye = (row == col).astype(F32)
        grams, inverses, mixes = [], [], []
        for slot in range(slots):
            total = gram_refs[0][slot]
            for ref in gram_refs[1:]:
                total = total + ref[slot]
            squares = jnp.sum(total * eye, keepdims=True)
            inverse = 1.0 / (jnp.sqrt(squares) + epsilon)
            grams.append(total * inverse * inverse)
            inverses.append(inverse)
            mixes.append(None)
        for step in range(ITERS):
            square = [product(gram, gram) for gram in grams]
            factor = [
                quintic_a * eye + quintic_b * gram + quintic_c * sq for gram, sq in zip(grams, square)
            ]
            mixes = [
                f if mix is None else product(mix, f) for mix, f in zip(mixes, factor)
            ]
            if step < ITERS - 1:
                half = [product(gram, f) for gram, f in zip(grams, factor)]
                grams = [product(h, f) for h, f in zip(half, factor)]
        for slot in range(slots):
            out_ref[slot] = mixes[slot] * (scale * inverses[slot])

    return pl.pallas_call(
        kernel,
        out_shape=jax.ShapeDtypeStruct((slots, HEAD, HEAD), F32),
        in_specs=[whole()] * len(grams),
        out_specs=whole(),
        compiler_params=params(),
        cost_estimate=cost(slots * 18 * 2 * 6 * HEAD**3, 4 * slots * HEAD * HEAD * 5),
        name="mixing",
    )(*grams)


def apply_mixing(buffer, mixes, slots):
    rows, width = buffer.shape
    count = lax.axis_size("dp")
    chips = count // CORES
    mats = width // HEAD
    span = slots * HEAD
    distances = [distance for distance, _ in mixes]

    def kernel(*refs):
        mix_refs = refs[: len(mixes)]
        buf_ref, out_ref = refs[len(mixes) :]
        own = lax.axis_index("dp")
        for distance, mix_ref in zip(distances, mix_refs):
            owner = own ^ distance
            place = (owner % CORES) * chips + owner // CORES

            @pl.when(place * slots < mats)
            def one():
                for slot in range(slots):
                    columns = pl.ds(pl.multiple_of(place * span + slot * HEAD, HEAD), HEAD)
                    values = buf_ref[:, columns]
                    mix = mix_ref[slot]
                    total = None
                    for part in range(3):
                        piece = mix.astype(BF16)
                        mix = mix - piece.astype(F32)
                        term = jnp.dot(values, piece, preferred_element_type=F32)
                        total = term if total is None else total + term
                    out_ref[:, columns] = total.astype(BF16)

    return pl.pallas_call(
        kernel,
        out_shape=jax.ShapeDtypeStruct((rows, width), BF16),
        in_specs=[whole()] * (len(mixes) + 1),
        out_specs=whole(),
        compiler_params=params(),
        cost_estimate=cost(6 * rows * width * HEAD, 4 * rows * width),
        name="apply_mixing",
    )(*[mix for _, mix in mixes], buffer)


def weight_product(kv_rows, weights):
    tokens, lat = kv_rows.shape
    width = weights.shape[0]
    span = width // CHUNKS
    block = span // 2 if span % 2 == 0 else span

    def kernel(kv_ref, w_ref, out_ref):
        out_ref[0] = lax.dot_general(
            kv_ref[...], w_ref[...], (((1,), (1,)), ((), ())), preferred_element_type=F32
        )

    parts = span // block
    return pl.pallas_call(
        kernel,
        grid=(CHUNKS, parts),
        out_shape=jax.ShapeDtypeStruct((CHUNKS, tokens, span), F32),
        in_specs=[
            pl.BlockSpec((tokens, lat), lambda i, j: (0, 0)),
            pl.BlockSpec((block, lat), lambda i, j: (i * parts + j, 0)),
        ],
        out_specs=pl.BlockSpec((1, tokens, block), lambda i, j: (i, 0, j)),
        compiler_params=params(),
        cost_estimate=cost(2 * tokens * lat * width, 2 * lat * (tokens + width) + 4 * tokens * width),
        name="weight_product",
    )(kv_rows, weights)


def relay_step(chunk, received, products, cotangent):
    chunks, tokens, span = products.shape

    def kernel(chunk_ref, *refs):
        out_ref = refs[-1]
        cot_ref, prod_ref = refs[-3], refs[-2]
        base = cot_ref[...]
        if received is not None:
            last = lax.axis_index("pipe") == lax.axis_size("pipe") - 1
            base = jnp.where(last, base, refs[0][...])
        out_ref[...] = (base.astype(F32) + prod_ref[0]).astype(BF16)

    first = [] if received is None else [received]
    return pl.pallas_call(
        kernel,
        grid_spec=pltpu.PrefetchScalarGridSpec(
            num_scalar_prefetch=1,
            grid=(1,),
            in_specs=[pl.BlockSpec((tokens, span), lambda i, c: (0, 0))] * len(first)
            + [
                pl.BlockSpec((tokens, span), lambda i, c: (0, c[0])),
                pl.BlockSpec((1, tokens, span), lambda i, c: (c[0], 0, 0)),
            ],
            out_specs=pl.BlockSpec((tokens, span), lambda i, c: (0, 0)),
        ),
        out_shape=jax.ShapeDtypeStruct((tokens, span), BF16),
        compiler_params=params(),
        cost_estimate=cost(tokens * span, 10 * tokens * span),
        name="relay_step",
    )(chunk, *first, cotangent, products)


def relay(kv_rows, weights, cotangent):
    products = weight_product(kv_rows, weights)
    sections = lax.axis_size("pipe")
    stage = lax.axis_index("pipe")
    sent = []
    moved = []
    for tick in range(CHUNKS + LAG * (sections - 1)):
        received = moved[tick - LAG] if tick >= LAG else None
        chunk = jnp.clip(tick - LAG * (sections - 1 - stage), 0, CHUNKS - 1)
        sent.append(relay_step(chunk.reshape(1).astype(jnp.int32), received, products, cotangent))
        if tick < CHUNKS + LAG * (sections - 2):
            moved.append(down(sent[-1]))
    outs = []
    for chunk in range(CHUNKS):
        choice = sent[chunk]
        for back in range(1, sections):
            choice = jnp.where(stage == sections - 1 - back, sent[chunk + LAG * back], choice)
        outs.append(choice)
    return jnp.concatenate(outs, axis=1)


def shards(acts, cotangent, kv_grads, w_kv, momentum):
    inputs, kv_rows, weights, moment = acts[0], kv_grads[0], w_kv[0], momentum[0]
    tokens, width = inputs.shape
    groups = lax.axis_size("dp")
    chips = groups // CORES
    mats = moment.shape[1] // HEAD
    slots = max(1, mats // groups)
    scale_grad = 1.0 / (tokens * groups)
    scale = 0.2 * math.sqrt(max(width, HEAD))

    kv_parts = gather_tokens(kv_rows)
    columns = split_columns(inputs)
    acts_parts = {}
    for distance in range(chips):
        piece = columns[distance] if distance == 0 else swap(columns[distance], CORES * distance)
        acts_parts[CORES * distance] = piece[0]
        acts_parts[CORES * distance + 1] = swap(piece[1], 1)
    parts = [(acts_parts[distance], pieces) for distance, pieces in kv_parts]
    outgoing = relay(kv_rows, weights, cotangent)

    buffer, mine, theirs = gradient(parts, moment, scale_grad, slots)
    sums = add_pairs(mine, swap(theirs, 1))
    grams = [sums[0]] + [swap(sums[d], CORES * d) for d in range(1, chips)]
    mix = mixing(grams, scale)
    mixes = [(0, mix)] + [(CORES * d, swap(mix, CORES * d)) for d in range(1, chips)]
    mixes = mixes + [(distance + 1, swap(value, 1)) for distance, value in mixes]
    update = apply_mixing(buffer, mixes, slots)
    return (update[None], outgoing[None])


def solution(mesh):
    in_specs = (
        P("pipe", "dp", None),
        P("dp", None),
        P("pipe", "dp", None),
        P("pipe", None, None),
        P("pipe", "dp", None),
    )
    out_specs = (P("pipe", "dp", None), P("pipe", "dp", None))
    return jax.shard_map(shards, mesh=mesh, in_specs=in_specs, out_specs=out_specs, check_vma=False)
```

```python
import functools
import math

import jax
import jax.numpy as jnp
from jax import lax
from jax.experimental import pallas as pl
from jax.experimental.pallas import tpu as pltpu
from jax.sharding import PartitionSpec as P

HEAD = 128
ITERS = 5
CORES = 2
CHUNKS = 4
LAG = 2
PAD = 8

momentum_rate = 0.95
quintic_a = 3.4445
quintic_b = -4.775
quintic_c = 2.0315
epsilon = 1e-07

F32 = jnp.float32
BF16 = jnp.bfloat16
ANY = pl.BlockSpec(memory_space=pl.ANY)


def cost(flops, moved):
    return pl.CostEstimate(flops=int(flops), bytes_accessed=int(moved), transcendentals=0)


def params(mib):
    return pltpu.CompilerParams(vmem_limit_bytes=mib * 1024 * 1024)


def after(value, *others):
    return lax.optimization_barrier((value, *others))[0]


def swap(value, by):
    count = lax.axis_size("dp")
    return lax.ppermute(value, "dp", [(i ^ by[i % CORES], i) for i in range(count)])


def down(value):
    count = lax.axis_size("pipe")
    return lax.ppermute(value, "pipe", [(i, i - 1) for i in range(1, count)])


def by_core(pair):
    own = lax.axis_index("dp")
    if pair[0] == pair[1]:
        return pair[0]
    return jnp.where(own % CORES == 0, pair[0], pair[1])


def split_columns(inputs, relations):
    count = lax.axis_size("dp")
    tokens, width = inputs.shape
    block = width // count

    def kernel(in_ref, *out_refs):
        own = lax.axis_index("dp")
        for relation, out_ref in zip(relations, out_refs):
            flipped = relation if relation[0] % CORES == 0 else relation[::-1]
            owner = own ^ by_core(flipped)
            if block % 128 == 0:
                columns = pl.ds(pl.multiple_of(owner * block, 128), block)
                out_ref[...] = in_ref[:, columns].T
            else:
                for other in range(count):
                    @pl.when(owner == other)
                    def store():
                        out_ref[...] = in_ref[:, other * block : (other + 1) * block].T

    shape = jax.ShapeDtypeStruct((block, tokens), BF16)
    return pl.pallas_call(
        kernel,
        grid=(1,),
        out_shape=[shape] * len(relations),
        in_specs=[pl.BlockSpec((tokens, width), lambda i: (0, 0))],
        out_specs=[pl.BlockSpec((block, tokens), lambda i: (0, 0))] * len(relations),
        compiler_params=params(16),
        cost_estimate=cost(0, 4 * tokens * width),
        name="split_columns",
    )(inputs)


def triangle():
    row = lax.broadcasted_iota(jnp.int32, (HEAD, HEAD), 0)
    col = lax.broadcasted_iota(jnp.int32, (HEAD, HEAD), 1)
    return row, col


def pack(mats):
    if len(mats) % 2:
        return jnp.concatenate(mats, axis=0)
    row, col = triangle()
    rows = []
    for first, second in zip(mats[::2], mats[1::2]):
        diagonal = jnp.sum(jnp.where(row == col, second, 0.0), axis=0, keepdims=True)
        rows.append(jnp.where(col >= row, first, second))
        rows.append(jnp.broadcast_to(diagonal, (PAD, HEAD)))
    return jnp.concatenate(rows, axis=0)


def packed_rows(slots):
    return slots * HEAD if slots % 2 else slots // 2 * (HEAD + PAD)


def unpack(packed, slots):
    if slots % 2:
        return [packed[i * HEAD : (i + 1) * HEAD] for i in range(slots)]
    row, col = triangle()
    mats = []
    for pair in range(slots // 2):
        at = pair * (HEAD + PAD)
        square = packed[at : at + HEAD]
        diagonal = packed[at + HEAD : at + HEAD + 1]
        other = square.T
        mats.append(jnp.where(col >= row, square, other))
        mats.append(jnp.where(col == row, diagonal, jnp.where(col < row, square, other)))
    return mats


def gradient(left, right, moment, scale, slots):
    rows, width = moment.shape
    count = lax.axis_size("dp")
    mats = width // HEAD
    owners = mats // slots
    per_step = 2 if owners % 2 == 0 else 1
    block = per_step * slots * HEAD
    tokens = sum(piece.shape[0] for piece in right)
    n_left, n_right = len(left), len(right)
    packed = packed_rows(slots)
    steps = owners // per_step

    def kernel(*refs):
        left_refs = refs[:n_left]
        right_refs = refs[n_left : n_left + n_right]
        mom_ref, buf_ref = refs[n_left + n_right : n_left + n_right + 2]
        gram_refs = refs[n_left + n_right + 2 : -2]
        held, grams = refs[-2:]
        step = pl.program_id(0)
        own = lax.axis_index("dp")

        @pl.when(step == 0)
        def load():
            at = 0
            for ref in left_refs:
                held[:, at : at + ref.shape[1]] = ref[...]
                at += ref.shape[1]
            if owners < count:
                grams[...] = jnp.zeros_like(grams)

        kv_block = jnp.concatenate([ref[...] for ref in right_refs], axis=0)
        grad = jnp.dot(held[...], kv_block, preferred_element_type=F32)
        buffer = (momentum_rate * mom_ref[...].astype(F32) + grad * scale).astype(BF16)
        buf_ref[...] = buffer
        for which in range(per_step):
            first = which * slots * HEAD
            values = buffer[:, first : first + slots * HEAD]
            gram = lax.dot_general(values, values, (((0,), (0,)), ((), ())), preferred_element_type=F32)
            spans = [slice(slot * HEAD, (slot + 1) * HEAD) for slot in range(slots)]
            owner = step * per_step + which
            grams[owner ^ own] = pack([gram[span, span] for span in spans])

        @pl.when(step == steps - 1)
        def store():
            for distance, ref in enumerate(gram_refs):
                ref[...] = grams[distance]

    column = lambda height: pl.BlockSpec((height, block), lambda j: (0, j))
    return pl.pallas_call(
        kernel,
        grid=(steps,),
        out_shape=[jax.ShapeDtypeStruct((rows, width), BF16)]
        + [jax.ShapeDtypeStruct((packed, HEAD), F32)] * count,
        in_specs=[pl.BlockSpec(a.shape, lambda j: (0, 0)) for a in left]
        + [column(piece.shape[0]) for piece in right]
        + [column(rows)],
        out_specs=[column(rows)] + [pl.BlockSpec((packed, HEAD), lambda j: (0, 0))] * count,
        scratch_shapes=[pltpu.VMEM((rows, tokens), BF16), pltpu.VMEM((count, packed, HEAD), F32)],
        compiler_params=params(24),
        cost_estimate=cost(2 * rows * tokens * width, 2 * tokens * (rows + width) + 4 * rows * width),
        name="gradient",
    )(*left, *right, moment)


def mixing(grams, scale, slots):
    highest = lax.Precision.HIGHEST

    def product(left, right):
        return jnp.dot(left, right, precision=highest, preferred_element_type=F32)

    def kernel(*refs):
        gram_refs, out_ref = refs[:-1], refs[-1]
        row, col = triangle()
        eye = (row == col).astype(F32)
        total = gram_refs[0][...]
        for ref in gram_refs[1:]:
            total = total + ref[...]
        grams, inverses, mixes = [], [], []
        for gram in unpack(total, slots):
            squares = jnp.sum(gram * eye, keepdims=True)
            inverse = 1.0 / (jnp.sqrt(squares) + epsilon)
            grams.append(gram * inverse * inverse)
            inverses.append(inverse)
            mixes.append(None)
        for step in range(ITERS):
            square = [product(gram, gram) for gram in grams]
            factor = [
                quintic_a * eye + quintic_b * gram + quintic_c * sq for gram, sq in zip(grams, square)
            ]
            mixes = [f if mix is None else product(mix, f) for mix, f in zip(mixes, factor)]
            if step < ITERS - 1:
                half = [product(gram, f) for gram, f in zip(grams, factor)]
                grams = [product(h, f) for h, f in zip(half, factor)]
        out_ref[...] = pack([mix * (scale * inverse) for mix, inverse in zip(mixes, inverses)])

    packed = packed_rows(slots)
    spec = pl.BlockSpec((packed, HEAD), lambda i: (0, 0))
    return pl.pallas_call(
        kernel,
        grid=(1,),
        out_shape=jax.ShapeDtypeStruct((packed, HEAD), F32),
        in_specs=[spec] * len(grams),
        out_specs=spec,
        compiler_params=params(16),
        cost_estimate=cost(slots * 18 * 2 * 6 * HEAD**3, 4 * slots * HEAD * HEAD * 9),
        name="mixing",
    )(*grams)


def apply_mixing(buffer, mixes, slots):
    rows, width = buffer.shape
    count = lax.axis_size("dp")
    mats = width // HEAD
    owners = mats // slots
    per_step = 2 if owners % 2 == 0 else 1
    span = slots * HEAD
    block = per_step * span
    packed = packed_rows(slots)

    def kernel(*refs):
        mix_refs = refs[:count]
        buf_ref, out_ref, held = refs[count:]
        own = lax.axis_index("dp")
        step = pl.program_id(0)

        @pl.when(step == 0)
        def load():
            for distance, ref in enumerate(mix_refs):
                held[distance] = ref[...]

        for which in range(per_step):
            parts = unpack(held[(step * per_step + which) ^ own], slots)
            zero = jnp.zeros((HEAD, HEAD), F32)
            mix = jnp.concatenate(
                [
                    jnp.concatenate([part if j == i else zero for j in range(slots)], axis=1)
                    for i, part in enumerate(parts)
                ],
                axis=0,
            )
            columns = slice(which * span, (which + 1) * span)
            values = buf_ref[:, columns]
            total = None
            for part in range(3):
                piece = mix.astype(BF16)
                mix = mix - piece.astype(F32)
                term = jnp.dot(values, piece, preferred_element_type=F32)
                total = term if total is None else total + term
            out_ref[:, columns] = total.astype(BF16)

    column = pl.BlockSpec((rows, block), lambda j: (0, j))
    return pl.pallas_call(
        kernel,
        grid=(owners // per_step,),
        out_shape=jax.ShapeDtypeStruct((rows, width), BF16),
        in_specs=[pl.BlockSpec((packed, HEAD), lambda j: (0, 0))] * count + [column],
        out_specs=column,
        scratch_shapes=[pltpu.VMEM((count, packed, HEAD), F32)],
        compiler_params=params(16),
        cost_estimate=cost(6 * rows * width * HEAD, 4 * rows * width),
        name="apply_mixing",
    )(*mixes, buffer)


def weight_product(chunk, kv_rows, weights, cotangent):
    tokens, lat = kv_rows.shape
    width = weights.shape[0]
    span = width // CHUNKS
    block = 256 if span % 256 == 0 else span
    pieces = span // block

    def kernel(kv_ref, cot_ref, w_ref, out_ref, held, sems):
        copies = []
        for piece in range(pieces):
            source = w_ref.at[pl.ds(chunk * span + piece * block, block)]
            copies.append(
                pltpu.make_async_copy(source, held.at[pl.ds(piece * block, block)], sems.at[piece])
            )
            copies[-1].start()
        last = lax.axis_index("pipe") == lax.axis_size("pipe") - 1
        for piece in range(pieces):
            columns = slice(piece * block, (piece + 1) * block)
            copies[piece].wait()
            out = lax.dot_general(
                kv_ref[...], held[columns], (((1,), (1,)), ((), ())), preferred_element_type=F32
            )
            out_ref[:, columns] = out + jnp.where(last, cot_ref[:, columns].astype(F32), 0.0)

    return pl.pallas_call(
        kernel,
        grid=(1,),
        out_shape=jax.ShapeDtypeStruct((tokens, span), F32),
        in_specs=[
            pl.BlockSpec((tokens, lat), lambda i: (0, 0)),
            pl.BlockSpec((tokens, span), lambda i: (0, chunk)),
            ANY,
        ],
        out_specs=pl.BlockSpec((tokens, span), lambda i: (0, 0)),
        scratch_shapes=[pltpu.VMEM((span, lat), BF16), pltpu.SemaphoreType.DMA((pieces,))],
        compiler_params=params(16),
        cost_estimate=cost(2 * tokens * lat * span, 2 * lat * (tokens + span) + 4 * tokens * span),
        name="weight_product",
    )(kv_rows, cotangent, weights)


def relay_step(tick, received, products):
    tokens, span = products[0].shape
    sections = lax.axis_size("pipe")
    held = [(s, tick - LAG * (sections - 1 - s)) for s in range(sections)]
    held = [(s, c) for s, c in held if 0 <= c < CHUNKS]
    used = [products[c] for _, c in held]
    first = [] if received is None else [received]

    def kernel(*refs):
        prod_refs = refs[len(first) : len(first) + len(used)]
        out_ref, prod, sem = refs[-3:]
        stage = lax.axis_index("pipe")
        for (section, _), ref in zip(held, prod_refs):
            @pl.when(stage == section)
            def one():
                copy = pltpu.make_async_copy(ref, prod, sem)
                copy.start()
                copy.wait()
                if first and section < sections - 1:
                    out_ref[...] = (refs[0][...].astype(F32) + prod[...]).astype(BF16)
                else:
                    out_ref[...] = prod[...].astype(BF16)

    block = pl.BlockSpec((tokens, span), lambda i: (0, 0))
    return pl.pallas_call(
        kernel,
        grid=(1,),
        in_specs=[block] * len(first) + [ANY] * len(used),
        out_specs=block,
        out_shape=jax.ShapeDtypeStruct((tokens, span), BF16),
        scratch_shapes=[pltpu.VMEM((tokens, span), F32), pltpu.SemaphoreType.DMA],
        compiler_params=params(8),
        cost_estimate=cost(tokens * span, 8 * tokens * span),
        name="relay_step",
    )(*first, *used)


def collect(sent):
    tokens, span = sent[0].shape
    sections = lax.axis_size("pipe")

    def kernel(*refs):
        sent_refs = refs[: len(sent)]
        out_ref, sems = refs[len(sent) :]
        stage = lax.axis_index("pipe")
        for section in range(sections):
            @pl.when(stage == section)
            def one():
                copies = []
                for chunk in range(CHUNKS):
                    ref = sent_refs[chunk + LAG * (sections - 1 - section)]
                    target = out_ref.at[:, pl.ds(chunk * span, span)]
                    copies.append(pltpu.make_async_copy(ref, target, sems.at[chunk]))
                    copies[-1].start()
                for copy in copies:
                    copy.wait()

    return pl.pallas_call(
        kernel,
        in_specs=[ANY] * len(sent),
        out_specs=ANY,
        out_shape=jax.ShapeDtypeStruct((tokens, span * CHUNKS), BF16),
        scratch_shapes=[pltpu.SemaphoreType.DMA((CHUNKS,))],
        compiler_params=params(8),
        cost_estimate=cost(0, 4 * tokens * span * CHUNKS),
        name="collect",
    )(*sent)


def token_relations():
    count = lax.axis_size("dp")
    chips = count // CORES
    if chips == 4:
        base = [(0, 0), (CORES, 2 * CORES), (2 * CORES, CORES), (3 * CORES, 3 * CORES)]
    else:
        base = [(CORES * d, CORES * d) for d in range(chips)]
    return base, [(b ^ 1, a ^ 1) for a, b in base]


def shards(acts, cotangent, kv_grads, w_kv, momentum):
    inputs, kv_rows, weights, moment = acts[0], kv_grads[0], w_kv[0], momentum[0]
    tokens, width = inputs.shape
    groups = lax.axis_size("dp")
    sections = lax.axis_size("pipe")
    chips = groups // CORES
    mats = moment.shape[1] // HEAD
    slots = max(1, mats // groups)
    scale_grad = 1.0 / (tokens * groups)
    scale = 0.2 * math.sqrt(max(width, HEAD))
    other_core = (1, 1)

    same, crossed = token_relations()
    relations = same + crossed
    ticks = CHUNKS + LAG * (sections - 1)
    products, sent, moved = [], [], []

    def product(chunk, rows):
        products.append(weight_product(chunk, rows, weights, cotangent))

    def relay(*others):
        tick = len(sent)
        received = moved[tick - LAG] if tick >= LAG else None
        if received is not None:
            if others:
                received = after(received, *others)
            sent.append(relay_step(tick, received, products))
        else:
            sent.append(relay_step(tick, None, products))
        if tick < ticks - LAG:
            moved.append(down(sent[-1]))

    near = [kv_rows, swap(kv_rows, same[1])]
    if chips == 4:
        near.append(swap(kv_rows, same[2]))
        near.append(swap(near[1], same[2]))
    else:
        near.extend(swap(kv_rows, relation) for relation in same[2:])

    product(0, kv_rows)
    relay()
    columns = split_columns(after(inputs, sent[0]), relations)
    left = [columns[0]] + [swap(c, r) for c, r in zip(columns[1:], relations[1:])]
    product(1, after(kv_rows, columns[0]))
    relay()
    for chunk in range(2, CHUNKS):
        product(chunk, after(kv_rows, sent[-1]))
    far = [swap(piece, other_core) for piece in near]
    while len(sent) < 5:
        relay(*products[-1:])

    outs = gradient(left, near + far, after(moment, sent[-1]), scale_grad, slots)
    buffer, grams = outs[0], outs[1:]
    grams = [grams[0]] + [swap(g, (d, d)) for d, g in enumerate(grams) if d]
    while len(sent) < 7:
        relay(outs[1])
    mix = mixing([after(grams[0], sent[-1])] + grams[1:], scale, slots)
    mixes = [mix] + [swap(mix, (d, d)) for d in range(1, groups)]
    while len(sent) < ticks:
        relay(mix)
    update = apply_mixing(after(buffer, sent[-2]), mixes, slots)
    outgoing = collect(sent)
    return (update[None], outgoing[None])


def solution(mesh):
    in_specs = (
        P("pipe", "dp", None),
        P("dp", None),
        P("pipe", "dp", None),
        P("pipe", None, None),
        P("pipe", "dp", None),
    )
    out_specs = (P("pipe", "dp", None), P("pipe", "dp", None))
    return jax.shard_map(shards, mesh=mesh, in_specs=in_specs, out_specs=out_specs, check_vma=False)
```

```python
import functools
import math

import jax
import jax.numpy as jnp
from jax import lax
from jax.experimental import pallas as pl
from jax.experimental.pallas import tpu as pltpu
from jax.sharding import PartitionSpec as P

HEAD = 128
ITERS = 5
CORES = 2
CHUNKS = 4
LAG = 2
PAD = 8

momentum_rate = 0.95
quintic_a = 3.4445
quintic_b = -4.775
quintic_c = 2.0315
epsilon = 1e-07

F32 = jnp.float32
BF16 = jnp.bfloat16
ANY = pl.BlockSpec(memory_space=pl.ANY)
HBM = pl.BlockSpec(memory_space=pltpu.HBM)
VMEM = pl.BlockSpec(memory_space=pltpu.VMEM)


def cost(flops, moved):
    return pl.CostEstimate(flops=1, bytes_accessed=1, transcendentals=0)


def params(mib):
    return pltpu.CompilerParams(vmem_limit_bytes=mib * 1024 * 1024)


def in_hbm(value):
    return pltpu.with_memory_space_constraint(value, pltpu.HBM)


def after(value, *others):
    return lax.optimization_barrier((value, *others))[0]


def swap(value, by):
    count = lax.axis_size("dp")
    return lax.ppermute(value, "dp", [(i ^ by[i % CORES], i) for i in range(count)])


def down(value):
    count = lax.axis_size("pipe")
    return lax.ppermute(value, "pipe", [(i, i - 1) for i in range(1, count)])


def by_core(pair):
    own = lax.axis_index("dp")
    if pair[0] == pair[1]:
        return pair[0]
    return jnp.where(own % CORES == 0, pair[0], pair[1])


def split_columns(inputs):
    count = lax.axis_size("dp")
    tokens, width = inputs.shape
    block = width // count

    def kernel(in_ref, out_ref):
        for owner in range(count):
            out_ref[owner] = in_ref[:, owner * block : (owner + 1) * block].T

    return pl.pallas_call(
        kernel,
        out_shape=jax.ShapeDtypeStruct((count, block, tokens), BF16),
        in_specs=[VMEM],
        out_specs=VMEM,
        compiler_params=params(16),
        cost_estimate=cost(0, 4 * tokens * width),
        name="split_columns",
    )(inputs)


def triangle():
    row = lax.broadcasted_iota(jnp.int32, (HEAD, HEAD), 0)
    col = lax.broadcasted_iota(jnp.int32, (HEAD, HEAD), 1)
    return row, col


def pack(mats):
    if len(mats) % 2:
        return jnp.concatenate(mats, axis=0)
    row, col = triangle()
    rows = []
    for first, second in zip(mats[::2], mats[1::2]):
        diagonal = jnp.sum(jnp.where(row == col, second, 0.0), axis=0, keepdims=True)
        rows.append(jnp.where(col >= row, first, second))
        rows.append(jnp.broadcast_to(diagonal, (PAD, HEAD)))
    return jnp.concatenate(rows, axis=0)


def packed_rows(slots):
    return slots * HEAD if slots % 2 else slots // 2 * (HEAD + PAD)


def unpack(packed, slots):
    if slots % 2:
        return [packed[i * HEAD : (i + 1) * HEAD] for i in range(slots)]
    row, col = triangle()
    mats = []
    for pair in range(slots // 2):
        at = pair * (HEAD + PAD)
        square = packed[at : at + HEAD]
        diagonal = packed[at + HEAD : at + HEAD + 1]
        other = square.T
        mats.append(jnp.where(col >= row, square, other))
        mats.append(jnp.where(col == row, diagonal, jnp.where(col < row, square, other)))
    return mats


def gradient(left, sources, right, moment, scale, slots):
    rows, width = moment.shape
    count = lax.axis_size("dp")
    chips = count // CORES
    mats = width // HEAD
    owners = mats // slots
    per_step = 2 if owners % 2 == 0 else 1
    block = per_step * slots * HEAD
    tokens = right[0].shape[0]
    n_right = len(right)
    packed = packed_rows(slots)
    steps = owners // per_step

    def kernel(*refs):
        left_ref = refs[0]
        right_refs = refs[1 : 1 + n_right]
        mom_ref, buf_ref, mine_ref, theirs_ref, held, grams = refs[1 + n_right :]
        step = pl.program_id(0)
        own = lax.axis_index("dp")

        @pl.when(step == 0)
        def load():
            for at, pair in enumerate(sources):
                held[:, at * tokens : (at + 1) * tokens] = left_ref[own ^ by_core(pair)]
            if owners < count:
                grams[...] = jnp.zeros_like(grams)

        kv_block = jnp.concatenate([ref[...] for ref in right_refs], axis=0)
        grad = jnp.dot(held[...], kv_block, preferred_element_type=F32)
        buffer = (momentum_rate * mom_ref[...].astype(F32) + grad * scale).astype(BF16)
        buf_ref[...] = buffer
        for which in range(per_step):
            first = which * slots * HEAD
            values = buffer[:, first : first + slots * HEAD]
            gram = lax.dot_general(values, values, (((0,), (0,)), ((), ())), preferred_element_type=F32)
            spans = [slice(slot * HEAD, (slot + 1) * HEAD) for slot in range(slots)]
            owner = step * per_step + which
            grams[owner ^ own] = pack([gram[span, span] for span in spans])

        @pl.when(step == steps - 1)
        def store():
            for chip in range(chips):
                mine_ref[chip] = grams[CORES * chip]
                theirs_ref[chip] = grams[CORES * chip + 1]

    column = lambda height: pl.BlockSpec((height, block), lambda j: (0, j))
    gram_shape = jax.ShapeDtypeStruct((chips, packed, HEAD), F32)
    gram_spec = pl.BlockSpec((chips, packed, HEAD), lambda j: (0, 0, 0))
    return pl.pallas_call(
        kernel,
        grid=(steps,),
        out_shape=[jax.ShapeDtypeStruct((rows, width), BF16), gram_shape, gram_shape],
        in_specs=[pl.BlockSpec(left.shape, lambda j: (0, 0, 0))] + [column(tokens)] * n_right + [column(rows)],
        out_specs=[column(rows), gram_spec, gram_spec],
        scratch_shapes=[pltpu.VMEM((rows, n_right * tokens), BF16), pltpu.VMEM((count, packed, HEAD), F32)],
        compiler_params=params(18),
        cost_estimate=cost(
            2 * rows * tokens * n_right * width, 2 * tokens * n_right * (rows + width) + 4 * rows * width
        ),
        name="gradient",
    )(in_hbm(left), *[in_hbm(piece) for piece in right], in_hbm(moment))


def add_pairs(first, second):
    chips = first.shape[0]

    def kernel(first_ref, second_ref, *out_refs):
        for distance in range(chips):
            out_refs[distance][...] = first_ref[distance] + second_ref[distance]

    return pl.pallas_call(
        kernel,
        out_shape=[jax.ShapeDtypeStruct(first.shape[1:], F32)] * chips,
        in_specs=[VMEM] * 2,
        out_specs=[VMEM] * chips,
        compiler_params=params(16),
        cost_estimate=cost(first.size, 12 * first.size),
        name="add_pairs",
    )(first, second)


def mixing(grams, scale, slots):
    highest = lax.Precision.HIGHEST

    def product(left, right):
        return jnp.dot(left, right, precision=highest, preferred_element_type=F32)

    def kernel(*refs):
        gram_refs, out_ref = refs[:-1], refs[-1]
        row, col = triangle()
        eye = (row == col).astype(F32)
        total = gram_refs[0][...]
        for ref in gram_refs[1:]:
            total = total + ref[...]
        grams, inverses, mixes = [], [], []
        for gram in unpack(total, slots):
            squares = jnp.sum(gram * eye, keepdims=True)
            inverse = 1.0 / (jnp.sqrt(squares) + epsilon)
            grams.append(gram * inverse * inverse)
            inverses.append(inverse)
            mixes.append(None)
        for step in range(ITERS):
            square = [product(gram, gram) for gram in grams]
            factor = [
                quintic_a * eye + quintic_b * gram + quintic_c * sq for gram, sq in zip(grams, square)
            ]
            mixes = [f if mix is None else product(mix, f) for mix, f in zip(mixes, factor)]
            if step < ITERS - 1:
                half = [product(gram, f) for gram, f in zip(grams, factor)]
                grams = [product(h, f) for h, f in zip(half, factor)]
        out_ref[...] = pack([mix * (scale * inverse) for mix, inverse in zip(mixes, inverses)])

    packed = packed_rows(slots)
    spec = pl.BlockSpec((packed, HEAD), lambda i: (0, 0))
    return pl.pallas_call(
        kernel,
        grid=(1,),
        out_shape=jax.ShapeDtypeStruct((packed, HEAD), F32),
        in_specs=[spec] * len(grams),
        out_specs=spec,
        compiler_params=params(16),
        cost_estimate=cost(slots * 18 * 2 * 6 * HEAD**3, 4 * slots * HEAD * HEAD * 9),
        name="mixing",
    )(*grams)


def apply_mixing(buffer, distances, mixes, slots):
    rows, width = buffer.shape
    count = lax.axis_size("dp")
    mats = width // HEAD
    owners = mats // slots
    per_step = 2 if owners % 2 == 0 else 1
    span = slots * HEAD
    block = per_step * span
    packed = packed_rows(slots)

    def kernel(*refs):
        mix_refs = refs[:count]
        buf_ref, out_ref, held = refs[count:]
        own = lax.axis_index("dp")
        step = pl.program_id(0)

        @pl.when(step == 0)
        def load():
            for distance, ref in zip(distances, mix_refs):
                held[distance] = ref[...]

        for which in range(per_step):
            parts = unpack(held[(step * per_step + which) ^ own], slots)
            zero = jnp.zeros((HEAD, HEAD), F32)
            mix = jnp.concatenate(
                [
                    jnp.concatenate([part if j == i else zero for j in range(slots)], axis=1)
                    for i, part in enumerate(parts)
                ],
                axis=0,
            )
            columns = slice(which * span, (which + 1) * span)
            values = buf_ref[:, columns]
            total = None
            for part in range(3):
                piece = mix.astype(BF16)
                mix = mix - piece.astype(F32)
                term = jnp.dot(values, piece, preferred_element_type=F32)
                total = term if total is None else total + term
            out_ref[:, columns] = total.astype(BF16)

    column = pl.BlockSpec((rows, block), lambda j: (0, j))
    return pl.pallas_call(
        kernel,
        grid=(owners // per_step,),
        out_shape=jax.ShapeDtypeStruct((rows, width), BF16),
        in_specs=[pl.BlockSpec((packed, HEAD), lambda j: (0, 0))] * count + [column],
        out_specs=column,
        scratch_shapes=[pltpu.VMEM((count, packed, HEAD), F32)],
        compiler_params=params(16),
        cost_estimate=cost(6 * rows * width * HEAD, 4 * rows * width),
        name="apply_mixing",
    )(*mixes, buffer)


def weight_products(chunks, kv_rows, weights):
    tokens, lat = kv_rows.shape
    width = weights.shape[0]
    span = width // CHUNKS
    block = span // 2 if span % 16 == 0 else span
    each = span // block
    first, pieces = chunks[0] * each, len(chunks) * each

    def kernel(kv_ref, w_ref, *refs):
        out_refs, (held, sems) = refs[: len(chunks)], refs[len(chunks) :]
        copies = []
        for piece in range(pieces):
            source = w_ref.at[pl.ds((first + piece) * block, block)]
            copies.append(
                pltpu.make_async_copy(source, held.at[pl.ds(piece * block, block)], sems.at[piece])
            )
            copies[-1].start()
        for piece in range(pieces):
            copies[piece].wait()
            columns = slice(piece % each * block, (piece % each + 1) * block)
            out_refs[piece // each][:, columns] = lax.dot_general(
                kv_ref[...],
                held[piece * block : (piece + 1) * block],
                (((1,), (1,)), ((), ())),
                preferred_element_type=F32,
            )

    return pl.pallas_call(
        kernel,
        out_shape=[jax.ShapeDtypeStruct((tokens, span), F32)] * len(chunks),
        in_specs=[VMEM, HBM],
        out_specs=[VMEM] * len(chunks),
        scratch_shapes=[pltpu.VMEM((pieces * block, lat), BF16), pltpu.SemaphoreType.DMA((pieces,))],
        compiler_params=params(18),
        cost_estimate=cost(2 * tokens * lat * span, 4 * span * lat),
        name="weight_products",
    )(kv_rows, in_hbm(weights))


def relay_step(tick, received, products, cotangent):
    tokens, span = products[0].shape
    sections = lax.axis_size("pipe")
    held = [(s, tick - LAG * (sections - 1 - s)) for s in range(sections)]
    held = [(s, c) for s, c in held if 0 <= c < CHUNKS]
    used = [products[c] for _, c in held]
    inputs = []
    if received is not None:
        inputs.append(received)
    if tick < CHUNKS:
        inputs.append(cotangent)

    def kernel(*refs):
        prod_refs = refs[len(inputs) : len(inputs) + len(used)]
        out_ref = refs[-1]
        stage = lax.axis_index("pipe")
        for (section, chunk), ref in zip(held, prod_refs):
            @pl.when(stage == section)
            def one():
                if section == sections - 1:
                    base = refs[len(inputs) - 1][:, chunk * span : (chunk + 1) * span]
                else:
                    base = refs[0][...]
                out_ref[...] = (base.astype(F32) + ref[...]).astype(BF16)

    return pl.pallas_call(
        kernel,
        in_specs=[VMEM] * (len(inputs) + len(used)),
        out_specs=VMEM,
        out_shape=jax.ShapeDtypeStruct((tokens, span), BF16),
        compiler_params=params(8),
        cost_estimate=cost(tokens * span, 8 * tokens * span),
        name="relay_step",
    )(*inputs, *used)


def collect(sent):
    tokens, span = sent[0].shape
    sections = lax.axis_size("pipe")

    def kernel(*refs):
        sent_refs = refs[: len(sent)]
        out_ref, sems = refs[len(sent) :]
        stage = lax.axis_index("pipe")
        for section in range(sections):
            ticks = [chunk + LAG * (sections - 1 - section) for chunk in range(CHUNKS)]

            @pl.when(stage == section)
            def one():
                copies = []
                for chunk, tick in enumerate(ticks):
                    if tick < len(sent):
                        target = out_ref.at[:, pl.ds(chunk * span, span)]
                        copies.append(pltpu.make_async_copy(sent_refs[tick], target, sems.at[chunk]))
                        copies[-1].start()
                for copy in copies:
                    copy.wait()

    return pl.pallas_call(
        kernel,
        in_specs=[VMEM] * len(sent),
        out_specs=ANY,
        out_shape=jax.ShapeDtypeStruct((tokens, span * CHUNKS), BF16),
        scratch_shapes=[pltpu.SemaphoreType.DMA((CHUNKS,))],
        compiler_params=params(8),
        cost_estimate=cost(0, 4 * tokens * span * CHUNKS),
        name="collect",
    )(*sent)


def final_step(chunk, received, product, collected):
    tokens, span = product.shape

    def kernel(in_ref, prod_ref, old_ref, out_ref, held, sem):
        del old_ref

        @pl.when(lax.axis_index("pipe") == 0)
        def one():
            held[...] = (in_ref[...].astype(F32) + prod_ref[...]).astype(BF16)
            copy = pltpu.make_async_copy(held, out_ref.at[:, pl.ds(chunk * span, span)], sem)
            copy.start()
            copy.wait()

    return pl.pallas_call(
        kernel,
        in_specs=[VMEM, VMEM, ANY],
        out_specs=ANY,
        out_shape=jax.ShapeDtypeStruct(collected.shape, BF16),
        scratch_shapes=[pltpu.VMEM((tokens, span), BF16), pltpu.SemaphoreType.DMA],
        input_output_aliases={2: 0},
        compiler_params=params(8),
        cost_estimate=cost(0, 4 * tokens * span),
        name="final_step",
    )(received, product, collected)


def token_relations():
    count = lax.axis_size("dp")
    chips = count // CORES
    if chips == 4:
        base = [(0, 0), (CORES, 2 * CORES), (2 * CORES, CORES), (3 * CORES, 3 * CORES)]
    else:
        base = [(CORES * d, CORES * d) for d in range(chips)]
    return base, [(b ^ 1, a ^ 1) for a, b in base]


def shards(acts, cotangent, kv_grads, w_kv, momentum):
    inputs, kv_rows, weights, moment = acts[0], kv_grads[0], w_kv[0], momentum[0]
    tokens, width = inputs.shape
    groups = lax.axis_size("dp")
    sections = lax.axis_size("pipe")
    chips = groups // CORES
    mats = moment.shape[1] // HEAD
    slots = max(1, mats // groups)
    scale_grad = 1.0 / (tokens * groups)
    scale = 0.2 * math.sqrt(max(width, HEAD))
    other_core = (1, 1)

    same, crossed = token_relations()
    ticks = CHUNKS + LAG * (sections - 1)
    sent, moved = [], []

    def relay(*others):
        tick = len(sent)
        received = moved[tick - LAG] if tick >= LAG else None
        if received is not None:
            received = after(received, sent[-1], *others)
        sent.append(relay_step(tick, received, products, cotangent))
        if tick < ticks - LAG:
            moved.append(down(sent[-1]))

    near = [kv_rows] + [swap(kv_rows, relation) for relation in same[1 : 3 if chips == 4 else chips]]
    far = [swap(kv_rows, other_core)]
    columns = split_columns(inputs)
    left = lax.all_to_all(columns, "dp", 0, 0, tiled=True)
    early = list(range(min(LAG, CHUNKS)))
    products = list(weight_products(early, after(kv_rows, columns), weights))
    relay()
    relay()
    near = near[:1] + [after(piece, sent[1]) for piece in near[1:]]
    far.extend(swap(piece, other_core) for piece in near[1:])
    if chips == 4:
        near.append(swap(near[1], same[2]))
    products += weight_products(list(range(LAG, CHUNKS)), after(kv_rows, sent[1]), weights)
    relay(products[-1])
    relay()
    if chips == 4:
        far.append(swap(after(near[-1], sent[3]), other_core))

    buffer, mine, theirs = gradient(
        left, same + crossed, near + far, after(moment, sent[3]), scale_grad, slots
    )
    received = swap(theirs, other_core)
    relay(buffer)
    relay(buffer)
    sums = add_pairs(after(mine, sent[5]), received)
    grams = [sums[0]] + [swap(sums[d], (CORES * d, CORES * d)) for d in range(1, chips)]
    mix = mixing(grams, scale, slots)
    mixes = [mix] + [swap(mix, (CORES * d, CORES * d)) for d in range(1, chips)]
    far_mixes = [swap(m, other_core) for m in mixes]
    relay(*mixes[1:])
    relay()
    distances = [CORES * d for d in range(chips)] + [CORES * d + 1 for d in range(chips)]
    outgoing = collect(sent)
    update = apply_mixing(after(buffer, sent[7]), distances, mixes + far_mixes, slots)
    for chunk in range(CHUNKS - LAG, CHUNKS):
        tick = chunk + LAG * (sections - 1)
        outgoing = final_step(chunk, after(moved[tick - LAG], update), products[chunk], outgoing)
    return (update[None], outgoing[None])


def solution(mesh):
    in_specs = (
        P("pipe", "dp", None),
        P("dp", None),
        P("pipe", "dp", None),
        P("pipe", None, None),
        P("pipe", "dp", None),
    )
    out_specs = (P("pipe", "dp", None), P("pipe", "dp", None))
    return jax.shard_map(shards, mesh=mesh, in_specs=in_specs, out_specs=out_specs, check_vma=False)
```

```python
import functools
import math

import jax
import jax.numpy as jnp
from jax import lax
from jax.experimental import pallas as pl
from jax.experimental.pallas import tpu as pltpu
from jax.sharding import PartitionSpec as P

HEAD = 128
ITERS = 5
CORES = 2
CHUNKS = 4
LAG = 2
PAD = 8

momentum_rate = 0.95
quintic_a = 3.4445
quintic_b = -4.775
quintic_c = 2.0315
epsilon = 1e-07

F32 = jnp.float32
BF16 = jnp.bfloat16
ANY = pl.BlockSpec(memory_space=pl.ANY)
HBM = pl.BlockSpec(memory_space=pltpu.HBM)
VMEM = pl.BlockSpec(memory_space=pltpu.VMEM)


def cost(flops, moved):
    return pl.CostEstimate(flops=1, bytes_accessed=1, transcendentals=0)


def params(mib):
    return pltpu.CompilerParams(vmem_limit_bytes=mib * 1024 * 1024)


def in_hbm(value):
    return pltpu.with_memory_space_constraint(value, pltpu.HBM)


def after(value, *others):
    return lax.optimization_barrier((value, *others))[0]


def swap(value, by):
    count = lax.axis_size("dp")
    return lax.ppermute(value, "dp", [(i ^ by[i % CORES], i) for i in range(count)])


def down(value):
    count = lax.axis_size("pipe")
    return lax.ppermute(value, "pipe", [(i, i - 1) for i in range(1, count)])


def by_core(pair):
    own = lax.axis_index("dp")
    if pair[0] == pair[1]:
        return pair[0]
    return jnp.where(own % CORES == 0, pair[0], pair[1])


def split_columns(inputs):
    count = lax.axis_size("dp")
    tokens, width = inputs.shape
    block = width // count

    def kernel(in_ref, out_ref):
        for owner in range(count):
            out_ref[owner] = in_ref[:, owner * block : (owner + 1) * block].T

    return pl.pallas_call(
        kernel,
        out_shape=jax.ShapeDtypeStruct((count, block, tokens), BF16),
        in_specs=[VMEM],
        out_specs=VMEM,
        compiler_params=params(16),
        cost_estimate=cost(0, 4 * tokens * width),
        name="split_columns",
    )(inputs)


def triangle():
    row = lax.broadcasted_iota(jnp.int32, (HEAD, HEAD), 0)
    col = lax.broadcasted_iota(jnp.int32, (HEAD, HEAD), 1)
    return row, col


def pack(mats):
    if len(mats) % 2:
        return jnp.concatenate(mats, axis=0)
    row, col = triangle()
    rows = []
    for first, second in zip(mats[::2], mats[1::2]):
        diagonal = jnp.sum(jnp.where(row == col, second, 0.0), axis=0, keepdims=True)
        rows.append(jnp.where(col >= row, first, second))
        rows.append(jnp.broadcast_to(diagonal, (PAD, HEAD)))
    return jnp.concatenate(rows, axis=0)


def packed_rows(slots):
    return slots * HEAD if slots % 2 else slots // 2 * (HEAD + PAD)


def unpack(packed, slots):
    if slots % 2:
        return [packed[i * HEAD : (i + 1) * HEAD] for i in range(slots)]
    row, col = triangle()
    mats = []
    for pair in range(slots // 2):
        at = pair * (HEAD + PAD)
        square = packed[at : at + HEAD]
        diagonal = packed[at + HEAD : at + HEAD + 1]
        other = square.T
        mats.append(jnp.where(col >= row, square, other))
        mats.append(jnp.where(col == row, diagonal, jnp.where(col < row, square, other)))
    return mats


def gradient(left, sources, right, moment, scale, slots):
    rows, width = moment.shape
    count = lax.axis_size("dp")
    chips = count // CORES
    mats = width // HEAD
    owners = mats // slots
    per_step = 2 if owners % 2 == 0 else 1
    block = per_step * slots * HEAD
    tokens = right[0].shape[0]
    n_right = len(right)
    packed = packed_rows(slots)
    steps = owners // per_step

    def kernel(*refs):
        left_ref = refs[0]
        right_refs = refs[1 : 1 + n_right]
        mom_ref, buf_ref, mine_ref, theirs_ref, held, grams = refs[1 + n_right :]
        step = pl.program_id(0)
        own = lax.axis_index("dp")

        @pl.when(step == 0)
        def load():
            for at, pair in enumerate(sources):
                held[:, at * tokens : (at + 1) * tokens] = left_ref[own ^ by_core(pair)]
            if owners < count:
                grams[...] = jnp.zeros_like(grams)

        kv_block = jnp.concatenate([ref[...] for ref in right_refs], axis=0)
        grad = jnp.dot(held[...], kv_block, preferred_element_type=F32)
        buffer = (momentum_rate * mom_ref[...].astype(F32) + grad * scale).astype(BF16)
        buf_ref[...] = buffer
        for which in range(per_step):
            first = which * slots * HEAD
            values = buffer[:, first : first + slots * HEAD]
            gram = lax.dot_general(values, values, (((0,), (0,)), ((), ())), preferred_element_type=F32)
            spans = [slice(slot * HEAD, (slot + 1) * HEAD) for slot in range(slots)]
            owner = step * per_step + which
            grams[owner ^ own] = pack([gram[span, span] for span in spans])

        @pl.when(step == steps - 1)
        def store():
            for chip in range(chips):
                mine_ref[chip] = grams[CORES * chip]
                theirs_ref[chip] = grams[CORES * chip + 1]

    column = lambda height: pl.BlockSpec((height, block), lambda j: (0, j))
    gram_shape = jax.ShapeDtypeStruct((chips, packed, HEAD), F32)
    gram_spec = pl.BlockSpec((chips, packed, HEAD), lambda j: (0, 0, 0))
    return pl.pallas_call(
        kernel,
        grid=(steps,),
        out_shape=[jax.ShapeDtypeStruct((rows, width), BF16), gram_shape, gram_shape],
        in_specs=[pl.BlockSpec(left.shape, lambda j: (0, 0, 0))] + [column(tokens)] * n_right + [column(rows)],
        out_specs=[column(rows), gram_spec, gram_spec],
        scratch_shapes=[pltpu.VMEM((rows, n_right * tokens), BF16), pltpu.VMEM((count, packed, HEAD), F32)],
        compiler_params=params(18),
        cost_estimate=cost(
            2 * rows * tokens * n_right * width, 2 * tokens * n_right * (rows + width) + 4 * rows * width
        ),
        name="gradient",
    )(in_hbm(left), *[in_hbm(piece) for piece in right], in_hbm(moment))


def add_pairs(first, second):
    chips = first.shape[0]

    def kernel(first_ref, second_ref, *out_refs):
        for distance in range(chips):
            out_refs[distance][...] = first_ref[distance] + second_ref[distance]

    return pl.pallas_call(
        kernel,
        out_shape=[jax.ShapeDtypeStruct(first.shape[1:], F32)] * chips,
        in_specs=[VMEM] * 2,
        out_specs=[VMEM] * chips,
        compiler_params=params(16),
        cost_estimate=cost(first.size, 12 * first.size),
        name="add_pairs",
    )(first, second)


def mixing(grams, scale, slots):
    highest = lax.Precision.HIGHEST

    def product(left, right):
        return jnp.dot(left, right, precision=highest, preferred_element_type=F32)

    def kernel(*refs):
        gram_refs, out_ref = refs[:-1], refs[-1]
        row, col = triangle()
        eye = (row == col).astype(F32)
        total = gram_refs[0][...]
        for ref in gram_refs[1:]:
            total = total + ref[...]
        grams, inverses, mixes = [], [], []
        for gram in unpack(total, slots):
            squares = jnp.sum(gram * eye, keepdims=True)
            inverse = 1.0 / (jnp.sqrt(squares) + epsilon)
            grams.append(gram * inverse * inverse)
            inverses.append(inverse)
            mixes.append(None)
        for step in range(ITERS):
            square = [product(gram, gram) for gram in grams]
            factor = [
                quintic_a * eye + quintic_b * gram + quintic_c * sq for gram, sq in zip(grams, square)
            ]
            mixes = [f if mix is None else product(mix, f) for mix, f in zip(mixes, factor)]
            if step < ITERS - 1:
                half = [product(gram, f) for gram, f in zip(grams, factor)]
                grams = [product(h, f) for h, f in zip(half, factor)]
        out_ref[...] = pack([mix * (scale * inverse) for mix, inverse in zip(mixes, inverses)])

    packed = packed_rows(slots)
    spec = pl.BlockSpec((packed, HEAD), lambda i: (0, 0))
    return pl.pallas_call(
        kernel,
        grid=(1,),
        out_shape=jax.ShapeDtypeStruct((packed, HEAD), F32),
        in_specs=[spec] * len(grams),
        out_specs=spec,
        compiler_params=params(16),
        cost_estimate=cost(slots * 18 * 2 * 6 * HEAD**3, 4 * slots * HEAD * HEAD * 9),
        name="mixing",
    )(*grams)


def apply_mixing(buffer, distances, mixes, slots, sent):
    rows, width = buffer.shape
    tokens, wide = sent[0].shape
    count = lax.axis_size("dp")
    sections = lax.axis_size("pipe")
    mats = width // HEAD
    owners = mats // slots
    per_step = 2 if owners % 2 == 0 else 1
    steps = owners // per_step
    span = slots * HEAD
    block = per_step * span
    packed = packed_rows(slots)

    def kernel(*refs):
        mix_refs = refs[:count]
        sent_refs = refs[count : count + len(sent)]
        buf_ref, out_ref, relayed_ref, held, sems = refs[count + len(sent) :]
        own = lax.axis_index("dp")
        stage = lax.axis_index("pipe")
        step = pl.program_id(0)

        def each_copy(act):
            for section in range(sections):
                @pl.when(stage == section)
                def one():
                    for chunk in range(CHUNKS):
                        tick = chunk + LAG * (sections - 1 - section)
                        if tick < len(sent):
                            target = relayed_ref.at[:, pl.ds(chunk * wide, wide)]
                            act(pltpu.make_async_copy(sent_refs[tick], target, sems.at[chunk]))

        @pl.when(step == 0)
        def load():
            each_copy(lambda copy: copy.start())
            for distance, ref in zip(distances, mix_refs):
                held[distance] = ref[...]

        for which in range(per_step):
            parts = unpack(held[(step * per_step + which) ^ own], slots)
            zero = jnp.zeros((HEAD, HEAD), F32)
            mix = jnp.concatenate(
                [
                    jnp.concatenate([part if j == i else zero for j in range(slots)], axis=1)
                    for i, part in enumerate(parts)
                ],
                axis=0,
            )
            columns = slice(which * span, (which + 1) * span)
            values = buf_ref[:, columns]
            total = None
            for part in range(3):
                piece = mix.astype(BF16)
                mix = mix - piece.astype(F32)
                term = jnp.dot(values, piece, preferred_element_type=F32)
                total = term if total is None else total + term
            out_ref[:, columns] = total.astype(BF16)

        @pl.when(step == steps - 1)
        def finish():
            each_copy(lambda copy: copy.wait())

    column = pl.BlockSpec((rows, block), lambda j: (0, j))
    return pl.pallas_call(
        kernel,
        grid=(steps,),
        out_shape=[
            jax.ShapeDtypeStruct((rows, width), BF16),
            jax.ShapeDtypeStruct((tokens, wide * CHUNKS), BF16),
        ],
        in_specs=[pl.BlockSpec((packed, HEAD), lambda j: (0, 0))] * count + [VMEM] * len(sent) + [column],
        out_specs=[column, ANY],
        scratch_shapes=[pltpu.VMEM((count, packed, HEAD), F32), pltpu.SemaphoreType.DMA((CHUNKS,))],
        compiler_params=params(16),
        cost_estimate=cost(6 * rows * width * HEAD, 4 * rows * width),
        name="apply_mixing",
    )(*mixes, *sent, buffer)


def weight_products(chunks, kv_rows, weights):
    tokens, lat = kv_rows.shape
    width = weights.shape[0]
    span = width // CHUNKS
    block = span // 2 if span % 16 == 0 else span
    each = span // block
    first, pieces = chunks[0] * each, len(chunks) * each

    def kernel(kv_ref, w_ref, *refs):
        out_refs, (held, sems) = refs[: len(chunks)], refs[len(chunks) :]
        copies = []
        for piece in range(pieces):
            source = w_ref.at[pl.ds((first + piece) * block, block)]
            copies.append(
                pltpu.make_async_copy(source, held.at[pl.ds(piece * block, block)], sems.at[piece])
            )
            copies[-1].start()
        for piece in range(pieces):
            copies[piece].wait()
            columns = slice(piece % each * block, (piece % each + 1) * block)
            out_refs[piece // each][:, columns] = lax.dot_general(
                kv_ref[...],
                held[piece * block : (piece + 1) * block],
                (((1,), (1,)), ((), ())),
                preferred_element_type=F32,
            )

    return pl.pallas_call(
        kernel,
        out_shape=[jax.ShapeDtypeStruct((tokens, span), F32)] * len(chunks),
        in_specs=[VMEM, HBM],
        out_specs=[VMEM] * len(chunks),
        scratch_shapes=[pltpu.VMEM((pieces * block, lat), BF16), pltpu.SemaphoreType.DMA((pieces,))],
        compiler_params=params(18),
        cost_estimate=cost(2 * tokens * lat * span, 4 * span * lat),
        name="weight_products",
    )(kv_rows, in_hbm(weights))


def relay_step(tick, received, products, cotangent):
    tokens, span = products[0].shape
    sections = lax.axis_size("pipe")
    held = [(s, tick - LAG * (sections - 1 - s)) for s in range(sections)]
    held = [(s, c) for s, c in held if 0 <= c < CHUNKS]
    used = [products[c] for _, c in held]
    inputs = []
    if received is not None:
        inputs.append(received)
    if tick < CHUNKS:
        inputs.append(cotangent)

    def kernel(*refs):
        prod_refs = refs[len(inputs) : len(inputs) + len(used)]
        out_ref = refs[-1]
        stage = lax.axis_index("pipe")
        for (section, chunk), ref in zip(held, prod_refs):
            @pl.when(stage == section)
            def one():
                if section == sections - 1:
                    base = refs[len(inputs) - 1][:, chunk * span : (chunk + 1) * span]
                else:
                    base = refs[0][...]
                out_ref[...] = (base.astype(F32) + ref[...]).astype(BF16)

    return pl.pallas_call(
        kernel,
        in_specs=[VMEM] * (len(inputs) + len(used)),
        out_specs=VMEM,
        out_shape=jax.ShapeDtypeStruct((tokens, span), BF16),
        compiler_params=params(8),
        cost_estimate=cost(tokens * span, 8 * tokens * span),
        name="relay_step",
    )(*inputs, *used)


def last_step(received, products, relayed):
    tokens, span = products[0].shape
    several = len(received)

    def kernel(*refs):
        in_refs, prod_refs = refs[:several], refs[several : 2 * several]
        out_ref, held, sems = refs[2 * several + 1 :]

        @pl.when(lax.axis_index("pipe") == 0)
        def one():
            copies = []
            for at in range(several):
                held[at] = (in_refs[at][...].astype(F32) + prod_refs[at][...]).astype(BF16)
                target = out_ref.at[:, pl.ds((CHUNKS - several + at) * span, span)]
                copies.append(pltpu.make_async_copy(held.at[at], target, sems.at[at]))
                copies[-1].start()
            for copy in copies:
                copy.wait()

    return pl.pallas_call(
        kernel,
        in_specs=[VMEM] * (2 * several) + [ANY],
        out_specs=ANY,
        out_shape=jax.ShapeDtypeStruct(relayed.shape, BF16),
        scratch_shapes=[pltpu.VMEM((several, tokens, span), BF16), pltpu.SemaphoreType.DMA((several,))],
        input_output_aliases={2 * several: 0},
        compiler_params=params(8),
        cost_estimate=cost(0, 4 * tokens * span),
        name="last_step",
    )(*received, *products, relayed)


def token_relations():
    count = lax.axis_size("dp")
    chips = count // CORES
    if chips == 4:
        base = [(0, 0), (CORES, 2 * CORES), (2 * CORES, CORES), (3 * CORES, 3 * CORES)]
    else:
        base = [(CORES * d, CORES * d) for d in range(chips)]
    return base, [(b ^ 1, a ^ 1) for a, b in base]


def shards(acts, cotangent, kv_grads, w_kv, momentum):
    inputs, kv_rows, weights, moment = acts[0], kv_grads[0], w_kv[0], momentum[0]
    tokens, width = inputs.shape
    groups = lax.axis_size("dp")
    sections = lax.axis_size("pipe")
    chips = groups // CORES
    mats = moment.shape[1] // HEAD
    slots = max(1, mats // groups)
    scale_grad = 1.0 / (tokens * groups)
    scale = 0.2 * math.sqrt(max(width, HEAD))
    other_core = (1, 1)

    same, crossed = token_relations()
    ticks = CHUNKS + LAG * (sections - 1)
    sent, moved = [], []

    def relay(*others):
        tick = len(sent)
        received = moved[tick - LAG] if tick >= LAG else None
        if received is not None:
            received = after(received, sent[-1], *others)
        sent.append(relay_step(tick, received, products, cotangent))
        if tick < ticks - LAG:
            moved.append(down(sent[-1]))

    near = [kv_rows] + [swap(kv_rows, relation) for relation in same[1 : 3 if chips == 4 else chips]]
    far = [swap(kv_rows, other_core)]
    columns = split_columns(inputs)
    left = lax.all_to_all(columns, "dp", 0, 0, tiled=True)
    early = list(range(min(LAG, CHUNKS)))
    products = list(weight_products(early, after(kv_rows, columns), weights))
    near = near[:1] + [after(piece, products[0]) for piece in near[1:]]
    products = [after(product, far[0], *near[1:]) for product in products]
    relay()
    relay()
    far.extend(swap(piece, other_core) for piece in near[1:])
    if chips == 4:
        near.append(swap(near[1], same[2]))
    products += weight_products(list(range(LAG, CHUNKS)), after(kv_rows, sent[1]), weights)
    relay(products[-1])
    if chips == 4:
        far.append(swap(after(near[-1], sent[2], moved[1]), other_core))

    buffer, mine, theirs = gradient(
        left, same + crossed, near + far, after(moment, sent[2]), scale_grad, slots
    )
    received = swap(theirs, other_core)
    relay(buffer)
    relay()
    sums = add_pairs(after(mine, sent[4]), received)
    grams = [sums[0]] + [swap(sums[d], (CORES * d, CORES * d)) for d in range(1, chips)]
    relay(*grams[1:])
    mix = mixing([after(grams[0], sent[5])] + grams[1:], scale, slots)
    mixes = [mix] + [swap(mix, (CORES * d, CORES * d)) for d in range(1, chips)]
    relay(mixes[1])
    far_mixes = [swap(m, other_core) for m in mixes]
    relay(*mixes[1:])
    distances = [CORES * d for d in range(chips)] + [CORES * d + 1 for d in range(chips)]
    update, outgoing = apply_mixing(
        after(buffer, sent[7]), distances, mixes + far_mixes, slots, sent
    )
    outgoing = last_step([after(m, update) for m in moved[-LAG:]], products[-LAG:], outgoing)
    return (update[None], outgoing[None])


def solution(mesh):
    in_specs = (
        P("pipe", "dp", None),
        P("dp", None),
        P("pipe", "dp", None),
        P("pipe", None, None),
        P("pipe", "dp", None),
    )
    out_specs = (P("pipe", "dp", None), P("pipe", "dp", None))
    return jax.shard_map(shards, mesh=mesh, in_specs=in_specs, out_specs=out_specs, check_vma=False)
```

```python
import functools
import math

import jax
import jax.numpy as jnp
from jax import lax
from jax.experimental import pallas as pl
from jax.experimental.pallas import tpu as pltpu
from jax.sharding import PartitionSpec as P

HEAD = 128
ITERS = 5
CORES = 2
CHUNKS = 4
LAG = 2
PAD = 8

momentum_rate = 0.95
quintic_a = 3.4445
quintic_b = -4.775
quintic_c = 2.0315
epsilon = 1e-07

F32 = jnp.float32
BF16 = jnp.bfloat16
ANY = pl.BlockSpec(memory_space=pl.ANY)
HBM = pl.BlockSpec(memory_space=pltpu.HBM)
VMEM = pl.BlockSpec(memory_space=pltpu.VMEM)


def cost(flops, moved):
    return pl.CostEstimate(flops=1, bytes_accessed=1, transcendentals=0)


def params(mib):
    return pltpu.CompilerParams(vmem_limit_bytes=mib * 1024 * 1024)


def in_hbm(value):
    return pltpu.with_memory_space_constraint(value, pltpu.HBM)


def after(value, *others):
    return lax.optimization_barrier((value, *others))[0]


def swap(value, by):
    count = lax.axis_size("dp")
    return lax.ppermute(value, "dp", [(i ^ by[i % CORES], i) for i in range(count)])


def cut(value, parts):
    rows, width = value.shape
    block = rows // parts

    def kernel(in_ref, *refs):
        sems = refs[parts]
        copies = []
        for part in range(parts):
            source = in_ref.at[pl.ds(part * block, block)]
            copies.append(pltpu.make_async_copy(source, refs[part], sems.at[part]))
            copies[-1].start()
        for copy in copies:
            copy.wait()

    return pl.pallas_call(
        kernel,
        out_shape=[jax.ShapeDtypeStruct((block, width), value.dtype)] * parts,
        in_specs=[ANY],
        out_specs=[ANY] * parts,
        scratch_shapes=[pltpu.SemaphoreType.DMA((parts,))],
        compiler_params=params(8),
        cost_estimate=cost(0, 4 * value.size),
        name="cut",
    )(value)


def join(values):
    def kernel(*refs):
        for at, ref in enumerate(refs[:-1]):
            refs[-1][at] = ref[...]

    shape = jax.ShapeDtypeStruct((len(values),) + values[0].shape, values[0].dtype)
    return pl.pallas_call(
        kernel,
        out_shape=shape,
        in_specs=[VMEM] * len(values),
        out_specs=VMEM,
        compiler_params=params(8),
        cost_estimate=cost(0, 8 * values[0].size),
        name="join",
    )(*values)


def down(value):
    count = lax.axis_size("pipe")
    return lax.ppermute(value, "pipe", [(i, i - 1) for i in range(1, count)])


def by_core(pair):
    own = lax.axis_index("dp")
    if pair[0] == pair[1]:
        return pair[0]
    return jnp.where(own % CORES == 0, pair[0], pair[1])


def split_columns(inputs):
    count = lax.axis_size("dp")
    tokens, width = inputs.shape
    block = width // count
    pieces = count if block % HEAD == 0 else 1
    part = width // pieces

    def kernel(in_ref, out_ref, held, turned, in_sems, out_sems):
        copies = []
        for piece in range(pieces):
            columns = pl.ds(piece * part, part)
            copies.append(
                pltpu.make_async_copy(in_ref.at[:, columns], held.at[:, columns], in_sems.at[piece])
            )
            copies[-1].start()
        stores = []
        for owner in range(count):
            if owner * pieces % count == 0:
                copies[owner * pieces // count].wait()
            turned[owner] = held[:, owner * block : (owner + 1) * block].T
            stores.append(pltpu.make_async_copy(turned.at[owner], out_ref.at[owner], out_sems.at[owner]))
            stores[-1].start()
        for store in stores:
            store.wait()

    return pl.pallas_call(
        kernel,
        out_shape=pltpu.HBM((count, block, tokens), BF16),
        in_specs=[HBM],
        out_specs=HBM,
        scratch_shapes=[
            pltpu.VMEM((tokens, width), BF16),
            pltpu.VMEM((count, block, tokens), BF16),
            pltpu.SemaphoreType.DMA((pieces,)),
            pltpu.SemaphoreType.DMA((count,)),
        ],
        compiler_params=params(8),
        cost_estimate=cost(0, 4 * tokens * width),
        name="split_columns",
    )(in_hbm(inputs))


def triangle():
    row = lax.broadcasted_iota(jnp.int32, (HEAD, HEAD), 0)
    col = lax.broadcasted_iota(jnp.int32, (HEAD, HEAD), 1)
    return row, col


def pack(mats):
    if len(mats) % 2:
        return jnp.concatenate(mats, axis=0)
    row, col = triangle()
    rows = []
    for first, second in zip(mats[::2], mats[1::2]):
        diagonal = jnp.sum(jnp.where(row == col, second, 0.0), axis=0, keepdims=True)
        rows.append(jnp.where(col >= row, first, second))
        rows.append(jnp.broadcast_to(diagonal, (PAD, HEAD)))
    return jnp.concatenate(rows, axis=0)


def packed_rows(slots):
    return slots * HEAD if slots % 2 else slots // 2 * (HEAD + PAD)


def unpack(packed, slots):
    if slots % 2:
        return [packed[i * HEAD : (i + 1) * HEAD] for i in range(slots)]
    row, col = triangle()
    mats = []
    for pair in range(slots // 2):
        at = pair * (HEAD + PAD)
        square = packed[at : at + HEAD]
        diagonal = packed[at + HEAD : at + HEAD + 1]
        other = square.T
        mats.append(jnp.where(col >= row, square, other))
        mats.append(jnp.where(col == row, diagonal, jnp.where(col < row, square, other)))
    return mats


def gradient(left, sources, right, moment, scale, slots):
    rows, width = moment.shape
    count = lax.axis_size("dp")
    chips = count // CORES
    mats = width // HEAD
    owners = mats // slots
    per_step = 2 if owners % 2 == 0 else 1
    block = per_step * slots * HEAD
    tokens = right[0].shape[0]
    total_tokens = sum(piece.shape[0] for piece in right)
    n_right = len(right)
    packed = packed_rows(slots)
    steps = owners // per_step

    def kernel(*refs):
        left_ref = refs[0]
        right_refs = refs[1 : 1 + n_right]
        mom_ref, buf_ref, mine_ref, theirs_ref, held, grams = refs[1 + n_right :]
        step = pl.program_id(0)
        own = lax.axis_index("dp")

        @pl.when(step == 0)
        def load():
            for at, pair in enumerate(sources):
                held[:, at * tokens : (at + 1) * tokens] = left_ref[own ^ by_core(pair)]
            if owners < count:
                grams[...] = jnp.zeros_like(grams)

        kv_block = jnp.concatenate([ref[...] for ref in right_refs], axis=0)
        grad = jnp.dot(held[...], kv_block, preferred_element_type=F32)
        buffer = (momentum_rate * mom_ref[...].astype(F32) + grad * scale).astype(BF16)
        buf_ref[...] = buffer
        for which in range(per_step):
            first = which * slots * HEAD
            values = buffer[:, first : first + slots * HEAD]
            gram = lax.dot_general(values, values, (((0,), (0,)), ((), ())), preferred_element_type=F32)
            spans = [slice(slot * HEAD, (slot + 1) * HEAD) for slot in range(slots)]
            owner = step * per_step + which
            grams[owner ^ own] = pack([gram[span, span] for span in spans])

        @pl.when(step == steps - 1)
        def store():
            for chip in range(chips):
                mine_ref[chip] = grams[CORES * chip]
                theirs_ref[chip] = grams[CORES * chip + 1]
            theirs_ref[chips] = jnp.zeros((packed, HEAD), F32)

    column = lambda height: pl.BlockSpec((height, block), lambda j: (0, j))
    gram_shape = jax.ShapeDtypeStruct((chips, packed, HEAD), F32)
    gram_spec = pl.BlockSpec((chips, packed, HEAD), lambda j: (0, 0, 0))
    other_shape = jax.ShapeDtypeStruct((chips + 1, packed, HEAD), F32)
    other_spec = pl.BlockSpec((chips + 1, packed, HEAD), lambda j: (0, 0, 0))
    return pl.pallas_call(
        kernel,
        grid=(steps,),
        out_shape=[jax.ShapeDtypeStruct((rows, width), BF16), gram_shape, other_shape],
        in_specs=[pl.BlockSpec(left.shape, lambda j: (0, 0, 0))] + [column(piece.shape[0]) for piece in right] + [column(rows)],
        out_specs=[column(rows), gram_spec, other_spec],
        scratch_shapes=[pltpu.VMEM((rows, total_tokens), BF16), pltpu.VMEM((count, packed, HEAD), F32)],
        compiler_params=params(18),
        cost_estimate=cost(
            2 * rows * total_tokens * width, 2 * total_tokens * (rows + width) + 4 * rows * width
        ),
        name="gradient",
    )(in_hbm(left), *[in_hbm(piece) for piece in right], in_hbm(moment))


def add_pairs(first, second):
    chips = first.shape[0]

    def kernel(first_ref, second_ref, *out_refs):
        for distance in range(chips):
            out_refs[distance][...] = first_ref[distance] + second_ref[distance]

    return pl.pallas_call(
        kernel,
        out_shape=[jax.ShapeDtypeStruct(first.shape[1:], F32)] * chips,
        in_specs=[VMEM] * 2,
        out_specs=[VMEM] * chips,
        compiler_params=params(16),
        cost_estimate=cost(first.size, 12 * first.size),
        name="add_pairs",
    )(first, second)


def mixing(grams, scale, slots):
    highest = lax.Precision.HIGHEST

    def product(left, right):
        return jnp.dot(left, right, precision=highest, preferred_element_type=F32)

    def kernel(*refs):
        gram_refs, out_ref = refs[:-1], refs[-1]
        row, col = triangle()
        eye = (row == col).astype(F32)
        total = gram_refs[0][...]
        for ref in gram_refs[1:]:
            total = total + ref[...]
        grams, inverses, mixes = [], [], []
        for gram in unpack(total, slots):
            squares = jnp.sum(gram * eye, keepdims=True)
            inverse = 1.0 / (jnp.sqrt(squares) + epsilon)
            grams.append(gram * inverse * inverse)
            inverses.append(inverse)
            mixes.append(None)
        for step in range(ITERS):
            square = [product(gram, gram) for gram in grams]
            factor = [
                quintic_a * eye + quintic_b * gram + quintic_c * sq for gram, sq in zip(grams, square)
            ]
            mixes = [f if mix is None else product(mix, f) for mix, f in zip(mixes, factor)]
            if step < ITERS - 1:
                half = [product(gram, f) for gram, f in zip(grams, factor)]
                grams = [product(h, f) for h, f in zip(half, factor)]
        out_ref[...] = pack([mix * (scale * inverse) for mix, inverse in zip(mixes, inverses)])

    packed = packed_rows(slots)
    spec = pl.BlockSpec((packed, HEAD), lambda i: (0, 0))
    return pl.pallas_call(
        kernel,
        grid=(1,),
        out_shape=jax.ShapeDtypeStruct((packed, HEAD), F32),
        in_specs=[spec] * len(grams),
        out_specs=spec,
        compiler_params=params(16),
        cost_estimate=cost(slots * 18 * 2 * 6 * HEAD**3, 4 * slots * HEAD * HEAD * 9),
        name="mixing",
    )(*grams)


def apply_mixing(buffer, near, other, far, slots, sent):
    rows, width = buffer.shape
    tokens, wide = sent[0].shape
    count = lax.axis_size("dp")
    sections = lax.axis_size("pipe")
    mats = width // HEAD
    owners = mats // slots
    per_step = 2 if owners % 2 == 0 else 1
    steps = owners // per_step
    span = slots * HEAD
    block = per_step * span
    packed = packed_rows(slots)

    def kernel(*refs):
        near_refs, other_ref, far_ref = refs[: len(near)], refs[len(near)], refs[len(near) + 1]
        sent_refs = refs[len(near) + 2 : len(near) + 2 + len(sent)]
        buf_ref, out_ref, relayed_ref, held, sems = refs[len(near) + 2 + len(sent) :]
        own = lax.axis_index("dp")
        stage = lax.axis_index("pipe")
        step = pl.program_id(0)

        def each_copy(act):
            for section in range(sections):
                @pl.when(stage == section)
                def one():
                    for chunk in range(CHUNKS):
                        tick = chunk + LAG * (sections - 1 - section)
                        if tick < len(sent):
                            target = relayed_ref.at[:, pl.ds(chunk * wide, wide)]
                            act(pltpu.make_async_copy(sent_refs[tick], target, sems.at[chunk]))

        @pl.when(step == 0)
        def load():
            each_copy(lambda copy: copy.start())
            for chip, ref in enumerate(near_refs):
                held[CORES * chip] = ref[...]
                held[CORES * chip + 1] = far_ref[chip] if chip else other_ref[...]

        for which in range(per_step):
            parts = unpack(held[(step * per_step + which) ^ own], slots)
            zero = jnp.zeros((HEAD, HEAD), F32)
            mix = jnp.concatenate(
                [
                    jnp.concatenate([part if j == i else zero for j in range(slots)], axis=1)
                    for i, part in enumerate(parts)
                ],
                axis=0,
            )
            columns = slice(which * span, (which + 1) * span)
            values = buf_ref[:, columns]
            total = None
            for part in range(3):
                piece = mix.astype(BF16)
                mix = mix - piece.astype(F32)
                term = jnp.dot(values, piece, preferred_element_type=F32)
                total = term if total is None else total + term
            out_ref[:, columns] = total.astype(BF16)

        @pl.when(step == steps - 1)
        def finish():
            each_copy(lambda copy: copy.wait())

    column = pl.BlockSpec((rows, block), lambda j: (0, j))
    return pl.pallas_call(
        kernel,
        grid=(steps,),
        out_shape=[
            jax.ShapeDtypeStruct((rows, width), BF16),
            jax.ShapeDtypeStruct((tokens, wide * CHUNKS), BF16),
        ],
        in_specs=[pl.BlockSpec((packed, HEAD), lambda j: (0, 0))] * (len(near) + 1)
        + [pl.BlockSpec(far.shape, lambda j: (0, 0, 0))]
        + [VMEM] * len(sent)
        + [column],
        out_specs=[column, ANY],
        scratch_shapes=[pltpu.VMEM((count, packed, HEAD), F32), pltpu.SemaphoreType.DMA((CHUNKS,))],
        compiler_params=params(16),
        cost_estimate=cost(6 * rows * width * HEAD, 4 * rows * width),
        name="apply_mixing",
    )(*near, other, far, *sent, buffer)


def weight_products(chunks, kv_rows, weights):
    tokens, lat = kv_rows.shape
    width = weights.shape[0]
    span = width // CHUNKS
    block = span // 2 if span % 16 == 0 else span
    each = span // block
    first, pieces = chunks[0] * each, len(chunks) * each

    def kernel(kv_ref, w_ref, *refs):
        out_refs, (held, sems) = refs[: len(chunks)], refs[len(chunks) :]
        copies = []
        for piece in range(pieces):
            source = w_ref.at[pl.ds((first + piece) * block, block)]
            copies.append(
                pltpu.make_async_copy(source, held.at[pl.ds(piece * block, block)], sems.at[piece])
            )
            copies[-1].start()
        for piece in range(pieces):
            copies[piece].wait()
            columns = slice(piece % each * block, (piece % each + 1) * block)
            out_refs[piece // each][:, columns] = lax.dot_general(
                kv_ref[...],
                held[piece * block : (piece + 1) * block],
                (((1,), (1,)), ((), ())),
                preferred_element_type=F32,
            )

    return pl.pallas_call(
        kernel,
        out_shape=[jax.ShapeDtypeStruct((tokens, span), F32)] * len(chunks),
        in_specs=[VMEM, HBM],
        out_specs=[VMEM] * len(chunks),
        scratch_shapes=[pltpu.VMEM((pieces * block, lat), BF16), pltpu.SemaphoreType.DMA((pieces,))],
        compiler_params=params(18),
        cost_estimate=cost(2 * tokens * lat * span, 4 * span * lat),
        name="weight_products",
    )(kv_rows, in_hbm(weights))


def relay_step(tick, received, products, cotangent):
    tokens, span = products[0].shape
    sections = lax.axis_size("pipe")
    held = [(s, tick - LAG * (sections - 1 - s)) for s in range(sections)]
    held = [(s, c) for s, c in held if 0 <= c < CHUNKS]
    used = [products[c] for _, c in held]
    inputs = []
    if received is not None:
        inputs.append(received)
    if tick < CHUNKS:
        inputs.append(cotangent)

    def kernel(*refs):
        prod_refs = refs[len(inputs) : len(inputs) + len(used)]
        out_ref = refs[-1]
        stage = lax.axis_index("pipe")
        for (section, chunk), ref in zip(held, prod_refs):
            @pl.when(stage == section)
            def one():
                if section == sections - 1:
                    base = refs[len(inputs) - 1][:, chunk * span : (chunk + 1) * span]
                else:
                    base = refs[0][...]
                out_ref[...] = (base.astype(F32) + ref[...]).astype(BF16)

    return pl.pallas_call(
        kernel,
        in_specs=[VMEM] * (len(inputs) + len(used)),
        out_specs=VMEM,
        out_shape=jax.ShapeDtypeStruct((tokens, span), BF16),
        compiler_params=params(8),
        cost_estimate=cost(tokens * span, 8 * tokens * span),
        name="relay_step",
    )(*inputs, *used)


def last_step(received, products, relayed):
    tokens, span = products[0].shape
    several = len(received)

    def kernel(*refs):
        in_refs, prod_refs = refs[:several], refs[several : 2 * several]
        out_ref, held, sems = refs[2 * several + 1 :]

        @pl.when(lax.axis_index("pipe") == 0)
        def one():
            copies = []
            for at in range(several):
                held[at] = (in_refs[at][...].astype(F32) + prod_refs[at][...]).astype(BF16)
                target = out_ref.at[:, pl.ds((CHUNKS - several + at) * span, span)]
                copies.append(pltpu.make_async_copy(held.at[at], target, sems.at[at]))
                copies[-1].start()
            for copy in copies:
                copy.wait()

    return pl.pallas_call(
        kernel,
        in_specs=[VMEM] * (2 * several) + [ANY],
        out_specs=ANY,
        out_shape=jax.ShapeDtypeStruct(relayed.shape, BF16),
        scratch_shapes=[pltpu.VMEM((several, tokens, span), BF16), pltpu.SemaphoreType.DMA((several,))],
        input_output_aliases={2 * several: 0},
        compiler_params=params(8),
        cost_estimate=cost(0, 4 * tokens * span),
        name="last_step",
    )(*received, *products, relayed)


def token_relations():
    count = lax.axis_size("dp")
    chips = count // CORES
    if chips == 4:
        base = [(0, 0), (CORES, 2 * CORES), (2 * CORES, CORES), (3 * CORES, 3 * CORES)]
    else:
        base = [(CORES * d, CORES * d) for d in range(chips)]
    return base, [(b ^ 1, a ^ 1) for a, b in base]


def shards(acts, cotangent, kv_grads, w_kv, momentum):
    inputs, kv_rows, weights, moment = acts[0], kv_grads[0], w_kv[0], momentum[0]
    tokens, width = inputs.shape
    groups = lax.axis_size("dp")
    sections = lax.axis_size("pipe")
    chips = groups // CORES
    mats = moment.shape[1] // HEAD
    slots = max(1, mats // groups)
    scale_grad = 1.0 / (tokens * groups)
    scale = 0.2 * math.sqrt(max(width, HEAD))
    other_core = (1, 1)

    same, crossed = token_relations()
    ticks = CHUNKS + LAG * (sections - 1)
    sent, moved = [], []

    def relay(*others):
        tick = len(sent)
        received = moved[tick - LAG] if tick >= LAG else None
        if received is not None:
            received = after(received, sent[-1], *others)
        sent.append(relay_step(tick, received, products, cotangent))
        if tick < ticks - LAG:
            moved.append(down(sent[-1]))

    near = [kv_rows] + [swap(kv_rows, relation) for relation in same[1 : 3 if chips == 4 else chips]]
    far = [swap(kv_rows, other_core)]
    columns = split_columns(inputs)
    left = lax.all_to_all(columns, "dp", 0, 0, tiled=True)
    early = list(range(min(LAG, CHUNKS)))
    products = list(weight_products(early, after(kv_rows, columns), weights))
    near = near[:1] + [after(piece, products[0]) for piece in near[1:]]
    products = [after(product, far[0], *near[1:]) for product in products]
    relay()
    relay()
    far.extend(swap(piece, other_core) for piece in near[1:])
    if chips == 4:
        near.append(swap(near[1], same[2]))
    products += weight_products(list(range(LAG, CHUNKS)), after(kv_rows, sent[1]), weights)
    relay(products[-1])
    relay()
    if chips == 4:
        far.extend(swap(piece, other_core) for piece in cut(after(near[-1], sent[2]), 2))

    buffer, mine, theirs = gradient(
        left, same + crossed, near + far, after(moment, sent[3]), scale_grad, slots
    )
    relay(buffer)
    received = swap(after(theirs, sent[4]), other_core)
    relay(theirs)
    sums = add_pairs(after(mine, sent[5]), received)
    grams = [sums[0]] + [swap(sums[d], (CORES * d, CORES * d)) for d in range(1, chips)]
    relay(*grams[1:])
    mix = mixing([after(grams[0], sent[6])] + grams[1:], scale, slots)
    mixes = [mix] + [swap(mix, (CORES * d, CORES * d)) for d in range(1, chips)]
    relay(mix)
    far_mix = swap(after(mix, moved[6]), other_core)
    far_mixes = swap(join(mixes), other_core)
    update, outgoing = apply_mixing(after(buffer, sent[7]), mixes, far_mix, far_mixes, slots, sent)
    outgoing = last_step([after(m, update) for m in moved[-LAG:]], products[-LAG:], outgoing)
    return (update[None], outgoing[None])


def solution(mesh):
    in_specs = (
        P("pipe", "dp", None),
        P("dp", None),
        P("pipe", "dp", None),
        P("pipe", None, None),
        P("pipe", "dp", None),
    )
    out_specs = (P("pipe", "dp", None), P("pipe", "dp", None))
    return jax.shard_map(shards, mesh=mesh, in_specs=in_specs, out_specs=out_specs, check_vma=False)
```

```python
import functools
import math

import jax
import jax.numpy as jnp
from jax import lax
from jax.experimental import pallas as pl
from jax.experimental.pallas import tpu as pltpu
from jax.sharding import PartitionSpec as P

HEAD = 128
ITERS = 5
CORES = 2
CHUNKS = 4
LAG = 2
PAD = 8

momentum_rate = 0.95
quintic_a = 3.4445
quintic_b = -4.775
quintic_c = 2.0315
epsilon = 1e-07

F32 = jnp.float32
BF16 = jnp.bfloat16
ANY = pl.BlockSpec(memory_space=pl.ANY)
HBM = pl.BlockSpec(memory_space=pltpu.HBM)
VMEM = pl.BlockSpec(memory_space=pltpu.VMEM)


def cost(flops, moved):
    return pl.CostEstimate(flops=1, bytes_accessed=1, transcendentals=0)


def params(mib):
    return pltpu.CompilerParams(vmem_limit_bytes=mib * 1024 * 1024)


def in_hbm(value):
    return pltpu.with_memory_space_constraint(value, pltpu.HBM)


def after(value, *others):
    return lax.optimization_barrier((value, *others))[0]


def swap(value, by):
    count = lax.axis_size("dp")
    return lax.ppermute(value, "dp", [(i ^ by[i % CORES], i) for i in range(count)])


def cut(value, parts):
    rows, width = value.shape
    block = rows // parts

    def kernel(in_ref, *refs):
        sems = refs[parts]
        copies = []
        for part in range(parts):
            source = in_ref.at[pl.ds(part * block, block)]
            copies.append(pltpu.make_async_copy(source, refs[part], sems.at[part]))
            copies[-1].start()
        for copy in copies:
            copy.wait()

    return pl.pallas_call(
        kernel,
        out_shape=[jax.ShapeDtypeStruct((block, width), value.dtype)] * parts,
        in_specs=[ANY],
        out_specs=[ANY] * parts,
        scratch_shapes=[pltpu.SemaphoreType.DMA((parts,))],
        compiler_params=params(8),
        cost_estimate=cost(0, 4 * value.size),
        name="cut",
    )(value)


def join(values):
    def kernel(*refs):
        for at, ref in enumerate(refs[:-1]):
            refs[-1][at] = ref[...]

    shape = jax.ShapeDtypeStruct((len(values),) + values[0].shape, values[0].dtype)
    return pl.pallas_call(
        kernel,
        out_shape=shape,
        in_specs=[VMEM] * len(values),
        out_specs=VMEM,
        compiler_params=params(8),
        cost_estimate=cost(0, 8 * values[0].size),
        name="join",
    )(*values)


def down(value):
    count = lax.axis_size("pipe")
    return lax.ppermute(value, "pipe", [(i, i - 1) for i in range(1, count)])


def by_core(pair):
    own = lax.axis_index("dp")
    if pair[0] == pair[1]:
        return pair[0]
    return jnp.where(own % CORES == 0, pair[0], pair[1])


def split_columns(inputs):
    count = lax.axis_size("dp")
    tokens, width = inputs.shape
    block = width // count
    pieces = count if block % HEAD == 0 else 1
    part = width // pieces

    def kernel(in_ref, out_ref, held, turned, in_sems, out_sems):
        copies = []
        for piece in range(pieces):
            columns = pl.ds(piece * part, part)
            copies.append(
                pltpu.make_async_copy(in_ref.at[:, columns], held.at[:, columns], in_sems.at[piece])
            )
            copies[-1].start()
        stores = []
        for owner in range(count):
            if owner * pieces % count == 0:
                copies[owner * pieces // count].wait()
            turned[owner] = held[:, owner * block : (owner + 1) * block].T
            stores.append(pltpu.make_async_copy(turned.at[owner], out_ref.at[owner], out_sems.at[owner]))
            stores[-1].start()
        for store in stores:
            store.wait()

    return pl.pallas_call(
        kernel,
        out_shape=pltpu.HBM((count, block, tokens), BF16),
        in_specs=[HBM],
        out_specs=HBM,
        scratch_shapes=[
            pltpu.VMEM((tokens, width), BF16),
            pltpu.VMEM((count, block, tokens), BF16),
            pltpu.SemaphoreType.DMA((pieces,)),
            pltpu.SemaphoreType.DMA((count,)),
        ],
        compiler_params=params(8),
        cost_estimate=cost(0, 4 * tokens * width),
        name="split_columns",
    )(in_hbm(inputs))


def triangle():
    row = lax.broadcasted_iota(jnp.int32, (HEAD, HEAD), 0)
    col = lax.broadcasted_iota(jnp.int32, (HEAD, HEAD), 1)
    return row, col


def pack(mats):
    if len(mats) % 2:
        return jnp.concatenate(mats, axis=0)
    row, col = triangle()
    rows = []
    for first, second in zip(mats[::2], mats[1::2]):
        diagonal = jnp.sum(jnp.where(row == col, second, 0.0), axis=0, keepdims=True)
        rows.append(jnp.where(col >= row, first, second))
        rows.append(jnp.broadcast_to(diagonal, (PAD, HEAD)))
    return jnp.concatenate(rows, axis=0)


def packed_rows(slots):
    return slots * HEAD if slots % 2 else slots // 2 * (HEAD + PAD)


def unpack(packed, slots):
    if slots % 2:
        return [packed[i * HEAD : (i + 1) * HEAD] for i in range(slots)]
    row, col = triangle()
    mats = []
    for pair in range(slots // 2):
        at = pair * (HEAD + PAD)
        square = packed[at : at + HEAD]
        diagonal = packed[at + HEAD : at + HEAD + 1]
        other = square.T
        mats.append(jnp.where(col >= row, square, other))
        mats.append(jnp.where(col == row, diagonal, jnp.where(col < row, square, other)))
    return mats


def gradient(left, sources, right, moment, scale, slots):
    rows, width = moment.shape
    count = lax.axis_size("dp")
    chips = count // CORES
    mats = width // HEAD
    owners = mats // slots
    per_step = next(n for n in (4, 2, 1) if owners % n == 0)
    block = per_step * slots * HEAD
    tokens = right[0].shape[0]
    total_tokens = sum(piece.shape[0] for piece in right)
    n_right = len(right)
    packed = packed_rows(slots)
    steps = owners // per_step

    def kernel(*refs):
        left_ref = refs[0]
        right_refs = refs[1 : 1 + n_right]
        mom_ref, buf_ref, mine_ref, theirs_ref, held, grams = refs[1 + n_right :]
        step = pl.program_id(0)
        own = lax.axis_index("dp")

        @pl.when(step == 0)
        def load():
            for at, pair in enumerate(sources):
                held[:, at * tokens : (at + 1) * tokens] = left_ref[own ^ by_core(pair)]
            if owners < count:
                grams[...] = jnp.zeros_like(grams)

        kv_block = jnp.concatenate([ref[...] for ref in right_refs], axis=0)
        grad = jnp.dot(held[...], kv_block, preferred_element_type=F32)
        buffer = (momentum_rate * mom_ref[...].astype(F32) + grad * scale).astype(BF16)
        buf_ref[...] = buffer
        for which in range(per_step):
            first = which * slots * HEAD
            values = buffer[:, first : first + slots * HEAD]
            gram = lax.dot_general(values, values, (((0,), (0,)), ((), ())), preferred_element_type=F32)
            spans = [slice(slot * HEAD, (slot + 1) * HEAD) for slot in range(slots)]
            owner = step * per_step + which
            grams[owner ^ own] = pack([gram[span, span] for span in spans])

        @pl.when(step == steps - 1)
        def store():
            for chip in range(chips):
                mine_ref[chip] = grams[CORES * chip]
                theirs_ref[chip] = grams[CORES * chip + 1]
            theirs_ref[chips] = jnp.zeros((packed, HEAD), F32)

    column = lambda height: pl.BlockSpec((height, block), lambda j: (0, j))
    gram_shape = jax.ShapeDtypeStruct((chips, packed, HEAD), F32)
    gram_spec = pl.BlockSpec((chips, packed, HEAD), lambda j: (0, 0, 0))
    other_shape = jax.ShapeDtypeStruct((chips + 1, packed, HEAD), F32)
    other_spec = pl.BlockSpec((chips + 1, packed, HEAD), lambda j: (0, 0, 0))
    return pl.pallas_call(
        kernel,
        grid=(steps,),
        out_shape=[jax.ShapeDtypeStruct((rows, width), BF16), gram_shape, other_shape],
        in_specs=[pl.BlockSpec(left.shape, lambda j: (0, 0, 0))] + [column(piece.shape[0]) for piece in right] + [column(rows)],
        out_specs=[column(rows), gram_spec, other_spec],
        scratch_shapes=[pltpu.VMEM((rows, total_tokens), BF16), pltpu.VMEM((count, packed, HEAD), F32)],
        compiler_params=params(26),
        cost_estimate=cost(
            2 * rows * total_tokens * width, 2 * total_tokens * (rows + width) + 4 * rows * width
        ),
        name="gradient",
    )(in_hbm(left), *[in_hbm(piece) for piece in right], in_hbm(moment))


def add_pairs(first, second):
    chips = first.shape[0]

    def kernel(first_ref, second_ref, *out_refs):
        for distance in range(chips):
            out_refs[distance][...] = first_ref[distance] + second_ref[distance]

    return pl.pallas_call(
        kernel,
        out_shape=[jax.ShapeDtypeStruct(first.shape[1:], F32)] * chips,
        in_specs=[VMEM] * 2,
        out_specs=[VMEM] * chips,
        compiler_params=params(16),
        cost_estimate=cost(first.size, 12 * first.size),
        name="add_pairs",
    )(first, second)


def mixing(grams, scale, slots):
    highest = lax.Precision.HIGHEST

    def product(left, right):
        return jnp.dot(left, right, precision=highest, preferred_element_type=F32)

    def kernel(*refs):
        gram_refs, out_ref = refs[:-1], refs[-1]
        row, col = triangle()
        eye = (row == col).astype(F32)
        total = gram_refs[0][...]
        for ref in gram_refs[1:]:
            total = total + ref[...]
        grams, inverses, mixes = [], [], []
        for gram in unpack(total, slots):
            squares = jnp.sum(gram * eye, keepdims=True)
            inverse = 1.0 / (jnp.sqrt(squares) + epsilon)
            grams.append(gram * inverse * inverse)
            inverses.append(inverse)
            mixes.append(None)
        for step in range(ITERS):
            square = [product(gram, gram) for gram in grams]
            factor = [
                quintic_a * eye + quintic_b * gram + quintic_c * sq for gram, sq in zip(grams, square)
            ]
            mixes = [f if mix is None else product(mix, f) for mix, f in zip(mixes, factor)]
            if step < ITERS - 1:
                half = [product(gram, f) for gram, f in zip(grams, factor)]
                grams = [product(h, f) for h, f in zip(half, factor)]
        out_ref[...] = pack([mix * (scale * inverse) for mix, inverse in zip(mixes, inverses)])

    packed = packed_rows(slots)
    spec = pl.BlockSpec((packed, HEAD), lambda i: (0, 0))
    return pl.pallas_call(
        kernel,
        grid=(1,),
        out_shape=jax.ShapeDtypeStruct((packed, HEAD), F32),
        in_specs=[spec] * len(grams),
        out_specs=spec,
        compiler_params=params(16),
        cost_estimate=cost(slots * 18 * 2 * 6 * HEAD**3, 4 * slots * HEAD * HEAD * 9),
        name="mixing",
    )(*grams)


def apply_mixing(buffer, near, other, far, slots, sent):
    rows, width = buffer.shape
    tokens, wide = sent[0].shape
    count = lax.axis_size("dp")
    sections = lax.axis_size("pipe")
    mats = width // HEAD
    owners = mats // slots
    per_step = 2 if owners % 2 == 0 else 1
    steps = owners // per_step
    span = slots * HEAD
    block = per_step * span
    packed = packed_rows(slots)

    def kernel(*refs):
        near_refs, other_ref, far_ref = refs[: len(near)], refs[len(near)], refs[len(near) + 1]
        sent_refs = refs[len(near) + 2 : len(near) + 2 + len(sent)]
        buf_ref, out_ref, relayed_ref, held, sems = refs[len(near) + 2 + len(sent) :]
        own = lax.axis_index("dp")
        stage = lax.axis_index("pipe")
        step = pl.program_id(0)

        def each_copy(act):
            for section in range(sections):
                @pl.when(stage == section)
                def one():
                    for chunk in range(CHUNKS):
                        tick = chunk + LAG * (sections - 1 - section)
                        if tick < len(sent):
                            target = relayed_ref.at[:, pl.ds(chunk * wide, wide)]
                            act(pltpu.make_async_copy(sent_refs[tick], target, sems.at[chunk]))

        @pl.when(step == 0)
        def load():
            each_copy(lambda copy: copy.start())
            for chip, ref in enumerate(near_refs):
                held[CORES * chip] = ref[...]
                held[CORES * chip + 1] = far_ref[chip] if chip else other_ref[...]

        for which in range(per_step):
            parts = unpack(held[(step * per_step + which) ^ own], slots)
            zero = jnp.zeros((HEAD, HEAD), F32)
            mix = jnp.concatenate(
                [
                    jnp.concatenate([part if j == i else zero for j in range(slots)], axis=1)
                    for i, part in enumerate(parts)
                ],
                axis=0,
            )
            columns = slice(which * span, (which + 1) * span)
            values = buf_ref[:, columns]
            total = None
            for part in range(3):
                piece = mix.astype(BF16)
                mix = mix - piece.astype(F32)
                term = jnp.dot(values, piece, preferred_element_type=F32)
                total = term if total is None else total + term
            out_ref[:, columns] = total.astype(BF16)

        @pl.when(step == steps - 1)
        def finish():
            each_copy(lambda copy: copy.wait())

    column = pl.BlockSpec((rows, block), lambda j: (0, j))
    return pl.pallas_call(
        kernel,
        grid=(steps,),
        out_shape=[
            jax.ShapeDtypeStruct((rows, width), BF16),
            jax.ShapeDtypeStruct((tokens, wide * CHUNKS), BF16),
        ],
        in_specs=[pl.BlockSpec((packed, HEAD), lambda j: (0, 0))] * (len(near) + 1)
        + [pl.BlockSpec(far.shape, lambda j: (0, 0, 0))]
        + [VMEM] * len(sent)
        + [column],
        out_specs=[column, ANY],
        scratch_shapes=[pltpu.VMEM((count, packed, HEAD), F32), pltpu.SemaphoreType.DMA((CHUNKS,))],
        compiler_params=params(16),
        cost_estimate=cost(6 * rows * width * HEAD, 4 * rows * width),
        name="apply_mixing",
    )(*near, other, far, *sent, buffer)


def weight_products(chunks, kv_rows, weights):
    tokens, lat = kv_rows.shape
    width = weights.shape[0]
    span = width // CHUNKS
    block = span // 2 if span % 16 == 0 else span
    each = span // block
    first, pieces = chunks[0] * each, len(chunks) * each

    def kernel(kv_ref, w_ref, *refs):
        out_refs, (held, sems) = refs[: len(chunks)], refs[len(chunks) :]
        copies = []
        for piece in range(pieces):
            source = w_ref.at[pl.ds((first + piece) * block, block)]
            copies.append(
                pltpu.make_async_copy(source, held.at[pl.ds(piece * block, block)], sems.at[piece])
            )
            copies[-1].start()
        for piece in range(pieces):
            copies[piece].wait()
            columns = slice(piece % each * block, (piece % each + 1) * block)
            out_refs[piece // each][:, columns] = lax.dot_general(
                kv_ref[...],
                held[piece * block : (piece + 1) * block],
                (((1,), (1,)), ((), ())),
                preferred_element_type=F32,
            )

    return pl.pallas_call(
        kernel,
        out_shape=[jax.ShapeDtypeStruct((tokens, span), F32)] * len(chunks),
        in_specs=[VMEM, HBM],
        out_specs=[VMEM] * len(chunks),
        scratch_shapes=[pltpu.VMEM((pieces * block, lat), BF16), pltpu.SemaphoreType.DMA((pieces,))],
        compiler_params=params(18),
        cost_estimate=cost(2 * tokens * lat * span, 4 * span * lat),
        name="weight_products",
    )(kv_rows, in_hbm(weights))


def relay_step(tick, received, products, cotangent):
    tokens, span = products[0].shape
    sections = lax.axis_size("pipe")
    held = [(s, tick - LAG * (sections - 1 - s)) for s in range(sections)]
    held = [(s, c) for s, c in held if 0 <= c < CHUNKS]
    used = [products[c] for _, c in held]
    inputs = []
    if received is not None:
        inputs.append(received)
    if tick < CHUNKS:
        inputs.append(cotangent)

    def kernel(*refs):
        prod_refs = refs[len(inputs) : len(inputs) + len(used)]
        out_ref = refs[-1]
        stage = lax.axis_index("pipe")
        for (section, chunk), ref in zip(held, prod_refs):
            @pl.when(stage == section)
            def one():
                if section == sections - 1:
                    base = refs[len(inputs) - 1][:, chunk * span : (chunk + 1) * span]
                else:
                    base = refs[0][...]
                out_ref[...] = (base.astype(F32) + ref[...]).astype(BF16)

    return pl.pallas_call(
        kernel,
        in_specs=[VMEM] * (len(inputs) + len(used)),
        out_specs=VMEM,
        out_shape=jax.ShapeDtypeStruct((tokens, span), BF16),
        compiler_params=params(8),
        cost_estimate=cost(tokens * span, 8 * tokens * span),
        name="relay_step",
    )(*inputs, *used)


def last_step(received, products, relayed):
    tokens, span = products[0].shape
    several = len(received)

    def kernel(*refs):
        in_refs, prod_refs = refs[:several], refs[several : 2 * several]
        out_ref, held, sems = refs[2 * several + 1 :]

        @pl.when(lax.axis_index("pipe") == 0)
        def one():
            copies = []
            for at in range(several):
                held[at] = (in_refs[at][...].astype(F32) + prod_refs[at][...]).astype(BF16)
                target = out_ref.at[:, pl.ds((CHUNKS - several + at) * span, span)]
                copies.append(pltpu.make_async_copy(held.at[at], target, sems.at[at]))
                copies[-1].start()
            for copy in copies:
                copy.wait()

    return pl.pallas_call(
        kernel,
        in_specs=[VMEM] * (2 * several) + [ANY],
        out_specs=ANY,
        out_shape=jax.ShapeDtypeStruct(relayed.shape, BF16),
        scratch_shapes=[pltpu.VMEM((several, tokens, span), BF16), pltpu.SemaphoreType.DMA((several,))],
        input_output_aliases={2 * several: 0},
        compiler_params=params(8),
        cost_estimate=cost(0, 4 * tokens * span),
        name="last_step",
    )(*received, *products, relayed)


def token_relations():
    count = lax.axis_size("dp")
    chips = count // CORES
    if chips == 4:
        base = [(0, 0), (CORES, 2 * CORES), (2 * CORES, CORES), (3 * CORES, 3 * CORES)]
    else:
        base = [(CORES * d, CORES * d) for d in range(chips)]
    return base, [(b ^ 1, a ^ 1) for a, b in base]


def shards(acts, cotangent, kv_grads, w_kv, momentum):
    inputs, kv_rows, weights, moment = acts[0], kv_grads[0], w_kv[0], momentum[0]
    tokens, width = inputs.shape
    groups = lax.axis_size("dp")
    sections = lax.axis_size("pipe")
    chips = groups // CORES
    mats = moment.shape[1] // HEAD
    slots = max(1, mats // groups)
    scale_grad = 1.0 / (tokens * groups)
    scale = 0.2 * math.sqrt(max(width, HEAD))
    other_core = (1, 1)

    same, crossed = token_relations()
    ticks = CHUNKS + LAG * (sections - 1)
    sent, moved = [], []

    def relay(*others):
        tick = len(sent)
        received = moved[tick - LAG] if tick >= LAG else None
        if received is not None:
            received = after(received, sent[-1], *others)
        sent.append(relay_step(tick, received, products, cotangent))
        if tick < ticks - LAG:
            moved.append(down(sent[-1]))

    near = [kv_rows] + [swap(kv_rows, relation) for relation in same[1 : 3 if chips == 4 else chips]]
    far = [swap(kv_rows, other_core)]
    columns = split_columns(inputs)
    left = lax.all_to_all(columns, "dp", 0, 0, tiled=True)
    products = list(weight_products([0], after(kv_rows, columns), weights))
    near = near[:1] + [after(piece, products[0]) for piece in near[1:]]
    products = [after(product, far[0], *near[1:]) for product in products]
    relay()
    products += weight_products([1], after(kv_rows, sent[0]), weights)
    relay()
    far.extend(swap(piece, other_core) for piece in near[1:])
    if chips == 4:
        near.append(swap(near[1], same[2]))
    products += weight_products(list(range(LAG, CHUNKS)), after(kv_rows, sent[1]), weights)
    relay(products[-1])
    relay()
    if chips == 4:
        far.extend(swap(piece, other_core) for piece in cut(after(near[-1], sent[2]), 2))

    buffer, mine, theirs = gradient(
        left, same + crossed, near + far, after(moment, sent[3]), scale_grad, slots
    )
    relay(buffer)
    received = swap(after(theirs, sent[4]), other_core)
    relay(theirs)
    sums = add_pairs(after(mine, sent[5]), received)
    grams = [sums[0]] + [swap(sums[d], (CORES * d, CORES * d)) for d in range(1, chips)]
    relay(*grams[1:])
    mix = mixing([after(grams[0], sent[6])] + grams[1:], scale, slots)
    mixes = [mix] + [swap(mix, (CORES * d, CORES * d)) for d in range(1, chips)]
    relay(mix)
    far_mix = swap(after(mix, moved[6]), other_core)
    far_mixes = swap(join(mixes), other_core)
    update, outgoing = apply_mixing(after(buffer, sent[7]), mixes, far_mix, far_mixes, slots, sent)
    outgoing = last_step([after(m, update) for m in moved[-LAG:]], products[-LAG:], outgoing)
    return (update[None], outgoing[None])


def solution(mesh):
    in_specs = (
        P("pipe", "dp", None),
        P("dp", None),
        P("pipe", "dp", None),
        P("pipe", None, None),
        P("pipe", "dp", None),
    )
    out_specs = (P("pipe", "dp", None), P("pipe", "dp", None))
    return jax.shard_map(shards, mesh=mesh, in_specs=in_specs, out_specs=out_specs, check_vma=False)
```

```python
import functools
import math

import jax
import jax.numpy as jnp
from jax import lax
from jax.experimental import pallas as pl
from jax.experimental.pallas import tpu as pltpu
from jax.sharding import PartitionSpec as P

HEAD = 128
ITERS = 5
CORES = 2
CHUNKS = 4
LAG = 2
PAD = 8

momentum_rate = 0.95
quintic_a = 3.4445
quintic_b = -4.775
quintic_c = 2.0315
epsilon = 1e-07

F32 = jnp.float32
BF16 = jnp.bfloat16
ANY = pl.BlockSpec(memory_space=pl.ANY)
HBM = pl.BlockSpec(memory_space=pltpu.HBM)
VMEM = pl.BlockSpec(memory_space=pltpu.VMEM)


def cost(flops, moved):
    return pl.CostEstimate(flops=1, bytes_accessed=1, transcendentals=0)


def params(mib):
    return pltpu.CompilerParams(vmem_limit_bytes=mib * 1024 * 1024)


def in_hbm(value):
    return pltpu.with_memory_space_constraint(value, pltpu.HBM)


def after(value, *others):
    return lax.optimization_barrier((value, *others))[0]


def swap(value, by):
    count = lax.axis_size("dp")
    return lax.ppermute(value, "dp", [(i ^ by[i % CORES], i) for i in range(count)])


def cut(value, parts):
    rows, width = value.shape
    block = rows // parts

    def kernel(in_ref, *refs):
        sems = refs[parts]
        copies = []
        for part in range(parts):
            source = in_ref.at[pl.ds(part * block, block)]
            copies.append(pltpu.make_async_copy(source, refs[part], sems.at[part]))
            copies[-1].start()
        for copy in copies:
            copy.wait()

    return pl.pallas_call(
        kernel,
        out_shape=[jax.ShapeDtypeStruct((block, width), value.dtype)] * parts,
        in_specs=[ANY],
        out_specs=[ANY] * parts,
        scratch_shapes=[pltpu.SemaphoreType.DMA((parts,))],
        compiler_params=params(8),
        cost_estimate=cost(0, 4 * value.size),
        name="cut",
    )(value)


def join(values):
    def kernel(*refs):
        for at, ref in enumerate(refs[:-1]):
            refs[-1][at] = ref[...]

    shape = jax.ShapeDtypeStruct((len(values),) + values[0].shape, values[0].dtype)
    return pl.pallas_call(
        kernel,
        out_shape=shape,
        in_specs=[VMEM] * len(values),
        out_specs=VMEM,
        compiler_params=params(8),
        cost_estimate=cost(0, 8 * values[0].size),
        name="join",
    )(*values)


def down(value):
    count = lax.axis_size("pipe")
    return lax.ppermute(value, "pipe", [(i, i - 1) for i in range(1, count)])


def by_core(pair):
    own = lax.axis_index("dp")
    if pair[0] == pair[1]:
        return pair[0]
    return jnp.where(own % CORES == 0, pair[0], pair[1])


def split_columns(inputs):
    count = lax.axis_size("dp")
    tokens, width = inputs.shape
    block = width // count
    pieces = count if block % HEAD == 0 else 1
    part = width // pieces

    def kernel(in_ref, out_ref, held, turned, in_sems, out_sems):
        copies = []
        for piece in range(pieces):
            columns = pl.ds(piece * part, part)
            copies.append(
                pltpu.make_async_copy(in_ref.at[:, columns], held.at[:, columns], in_sems.at[piece])
            )
            copies[-1].start()
        stores = []
        for owner in range(count):
            if owner * pieces % count == 0:
                copies[owner * pieces // count].wait()
            turned[owner] = held[:, owner * block : (owner + 1) * block].T
            stores.append(pltpu.make_async_copy(turned.at[owner], out_ref.at[owner], out_sems.at[owner]))
            stores[-1].start()
        for store in stores:
            store.wait()

    return pl.pallas_call(
        kernel,
        out_shape=pltpu.HBM((count, block, tokens), BF16),
        in_specs=[HBM],
        out_specs=HBM,
        scratch_shapes=[
            pltpu.VMEM((tokens, width), BF16),
            pltpu.VMEM((count, block, tokens), BF16),
            pltpu.SemaphoreType.DMA((pieces,)),
            pltpu.SemaphoreType.DMA((count,)),
        ],
        compiler_params=params(8),
        cost_estimate=cost(0, 4 * tokens * width),
        name="split_columns",
    )(in_hbm(inputs))


def triangle():
    row = lax.broadcasted_iota(jnp.int32, (HEAD, HEAD), 0)
    col = lax.broadcasted_iota(jnp.int32, (HEAD, HEAD), 1)
    return row, col


def pack(mats):
    if len(mats) % 2:
        return jnp.concatenate(mats, axis=0)
    row, col = triangle()
    rows = []
    for first, second in zip(mats[::2], mats[1::2]):
        diagonal = jnp.sum(jnp.where(row == col, second, 0.0), axis=0, keepdims=True)
        rows.append(jnp.where(col >= row, first, second))
        rows.append(jnp.broadcast_to(diagonal, (PAD, HEAD)))
    return jnp.concatenate(rows, axis=0)


def packed_rows(slots):
    return slots * HEAD if slots % 2 else slots // 2 * (HEAD + PAD)


def unpack(packed, slots):
    if slots % 2:
        return [packed[i * HEAD : (i + 1) * HEAD] for i in range(slots)]
    row, col = triangle()
    mats = []
    for pair in range(slots // 2):
        at = pair * (HEAD + PAD)
        square = packed[at : at + HEAD]
        diagonal = packed[at + HEAD : at + HEAD + 1]
        other = square.T
        mats.append(jnp.where(col >= row, square, other))
        mats.append(jnp.where(col == row, diagonal, jnp.where(col < row, square, other)))
    return mats


def gradient(left, sources, right, moment, scale, slots):
    rows, width = moment.shape
    count = lax.axis_size("dp")
    chips = count // CORES
    mats = width // HEAD
    owners = mats // slots
    per_step = next(n for n in (4, 2, 1) if owners % n == 0)
    block = per_step * slots * HEAD
    tokens = right[0].shape[0]
    total_tokens = sum(piece.shape[0] for piece in right)
    n_right = len(right)
    packed = packed_rows(slots)
    steps = owners // per_step

    def kernel(*refs):
        left_ref = refs[0]
        right_refs = refs[1 : 1 + n_right]
        mom_ref, buf_ref, mine_ref, theirs_ref, held, grams = refs[1 + n_right :]
        step = pl.program_id(0)
        own = lax.axis_index("dp")

        @pl.when(step == 0)
        def load():
            for at, pair in enumerate(sources):
                held[:, at * tokens : (at + 1) * tokens] = left_ref[own ^ by_core(pair)]
            if owners < count:
                grams[...] = jnp.zeros_like(grams)

        kv_block = jnp.concatenate([ref[...] for ref in right_refs], axis=0)
        grad = jnp.dot(held[...], kv_block, preferred_element_type=F32)
        buffer = (momentum_rate * mom_ref[...].astype(F32) + grad * scale).astype(BF16)
        buf_ref[...] = buffer
        for which in range(per_step):
            first = which * slots * HEAD
            values = buffer[:, first : first + slots * HEAD]
            gram = lax.dot_general(values, values, (((0,), (0,)), ((), ())), preferred_element_type=F32)
            spans = [slice(slot * HEAD, (slot + 1) * HEAD) for slot in range(slots)]
            owner = step * per_step + which
            grams[owner ^ own] = pack([gram[span, span] for span in spans])

        @pl.when(step == steps - 1)
        def store():
            for chip in range(chips):
                mine_ref[chip] = grams[CORES * chip]
                theirs_ref[chip] = grams[CORES * chip + 1]
            theirs_ref[chips] = jnp.zeros((packed, HEAD), F32)

    column = lambda height: pl.BlockSpec((height, block), lambda j: (0, j))
    gram_shape = jax.ShapeDtypeStruct((chips, packed, HEAD), F32)
    gram_spec = pl.BlockSpec((chips, packed, HEAD), lambda j: (0, 0, 0))
    other_shape = jax.ShapeDtypeStruct((chips + 1, packed, HEAD), F32)
    other_spec = pl.BlockSpec((chips + 1, packed, HEAD), lambda j: (0, 0, 0))
    return pl.pallas_call(
        kernel,
        grid=(steps,),
        out_shape=[jax.ShapeDtypeStruct((rows, width), BF16), gram_shape, other_shape],
        in_specs=[pl.BlockSpec(left.shape, lambda j: (0, 0, 0))] + [column(piece.shape[0]) for piece in right] + [column(rows)],
        out_specs=[column(rows), gram_spec, other_spec],
        scratch_shapes=[pltpu.VMEM((rows, total_tokens), BF16), pltpu.VMEM((count, packed, HEAD), F32)],
        compiler_params=params(26),
        cost_estimate=cost(
            2 * rows * total_tokens * width, 2 * total_tokens * (rows + width) + 4 * rows * width
        ),
        name="gradient",
    )(in_hbm(left), *[in_hbm(piece) for piece in right[:-2]], *right[-2:], in_hbm(moment))


def add_pairs(first, second):
    chips = first.shape[0]

    def kernel(first_ref, second_ref, *out_refs):
        for distance in range(chips):
            out_refs[distance][...] = first_ref[distance] + second_ref[distance]

    return pl.pallas_call(
        kernel,
        out_shape=[jax.ShapeDtypeStruct(first.shape[1:], F32)] * chips,
        in_specs=[VMEM] * 2,
        out_specs=[VMEM] * chips,
        compiler_params=params(16),
        cost_estimate=cost(first.size, 12 * first.size),
        name="add_pairs",
    )(first, second)


def mixing(grams, scale, slots):
    highest = lax.Precision.HIGHEST

    def product(left, right):
        return jnp.dot(left, right, precision=highest, preferred_element_type=F32)

    def kernel(*refs):
        gram_refs, out_ref = refs[:-1], refs[-1]
        row, col = triangle()
        eye = (row == col).astype(F32)
        total = gram_refs[0][...]
        for ref in gram_refs[1:]:
            total = total + ref[...]
        grams, inverses, mixes = [], [], []
        for gram in unpack(total, slots):
            squares = jnp.sum(gram * eye, keepdims=True)
            inverse = 1.0 / (jnp.sqrt(squares) + epsilon)
            grams.append(gram * inverse * inverse)
            inverses.append(inverse)
            mixes.append(None)
        for step in range(ITERS):
            square = [product(gram, gram) for gram in grams]
            factor = [
                quintic_a * eye + quintic_b * gram + quintic_c * sq for gram, sq in zip(grams, square)
            ]
            mixes = [f if mix is None else product(mix, f) for mix, f in zip(mixes, factor)]
            if step < ITERS - 1:
                half = [product(gram, f) for gram, f in zip(grams, factor)]
                grams = [product(h, f) for h, f in zip(half, factor)]
        out_ref[...] = pack([mix * (scale * inverse) for mix, inverse in zip(mixes, inverses)])

    packed = packed_rows(slots)
    spec = pl.BlockSpec((packed, HEAD), lambda i: (0, 0))
    return pl.pallas_call(
        kernel,
        grid=(1,),
        out_shape=jax.ShapeDtypeStruct((packed, HEAD), F32),
        in_specs=[spec] * len(grams),
        out_specs=spec,
        compiler_params=params(16),
        cost_estimate=cost(slots * 18 * 2 * 6 * HEAD**3, 4 * slots * HEAD * HEAD * 9),
        name="mixing",
    )(*grams)


def apply_mixing(buffer, near, other, far, slots, sent):
    rows, width = buffer.shape
    tokens, wide = sent[0].shape
    count = lax.axis_size("dp")
    sections = lax.axis_size("pipe")
    mats = width // HEAD
    owners = mats // slots
    per_step = next(n for n in (4, 2, 1) if owners % n == 0)
    steps = owners // per_step
    span = slots * HEAD
    block = per_step * span
    packed = packed_rows(slots)

    def kernel(*refs):
        near_refs, other_ref, far_ref = refs[: len(near)], refs[len(near)], refs[len(near) + 1]
        sent_refs = refs[len(near) + 2 : len(near) + 2 + len(sent)]
        buf_ref, out_ref, relayed_ref, held, sems = refs[len(near) + 2 + len(sent) :]
        own = lax.axis_index("dp")
        stage = lax.axis_index("pipe")
        step = pl.program_id(0)

        def each_copy(act):
            for section in range(sections):
                @pl.when(stage == section)
                def one():
                    for chunk in range(CHUNKS):
                        tick = chunk + LAG * (sections - 1 - section)
                        if tick < len(sent):
                            target = relayed_ref.at[:, pl.ds(chunk * wide, wide)]
                            act(pltpu.make_async_copy(sent_refs[tick], target, sems.at[chunk]))

        @pl.when(step == 0)
        def load():
            each_copy(lambda copy: copy.start())
            for chip, ref in enumerate(near_refs):
                held[CORES * chip] = ref[...]
                held[CORES * chip + 1] = far_ref[chip] if chip else other_ref[...]

        for which in range(per_step):
            parts = unpack(held[(step * per_step + which) ^ own], slots)
            zero = jnp.zeros((HEAD, HEAD), F32)
            mix = jnp.concatenate(
                [
                    jnp.concatenate([part if j == i else zero for j in range(slots)], axis=1)
                    for i, part in enumerate(parts)
                ],
                axis=0,
            )
            columns = slice(which * span, (which + 1) * span)
            values = buf_ref[:, columns]
            total = None
            for part in range(3):
                piece = mix.astype(BF16)
                mix = mix - piece.astype(F32)
                term = jnp.dot(values, piece, preferred_element_type=F32)
                total = term if total is None else total + term
            out_ref[:, columns] = total.astype(BF16)

        @pl.when(step == steps - 1)
        def finish():
            each_copy(lambda copy: copy.wait())

    column = pl.BlockSpec((rows, block), lambda j: (0, j))
    return pl.pallas_call(
        kernel,
        grid=(steps,),
        out_shape=[
            jax.ShapeDtypeStruct((rows, width), BF16),
            jax.ShapeDtypeStruct((tokens, wide * CHUNKS), BF16),
        ],
        in_specs=[pl.BlockSpec((packed, HEAD), lambda j: (0, 0))] * (len(near) + 1)
        + [pl.BlockSpec(far.shape, lambda j: (0, 0, 0))]
        + [VMEM] * len(sent)
        + [column],
        out_specs=[column, ANY],
        scratch_shapes=[pltpu.VMEM((count, packed, HEAD), F32), pltpu.SemaphoreType.DMA((CHUNKS,))],
        compiler_params=params(16),
        cost_estimate=cost(6 * rows * width * HEAD, 4 * rows * width),
        name="apply_mixing",
    )(*near, other, far, *sent, buffer)


def weight_products(chunks, kv_rows, weights):
    tokens, lat = kv_rows.shape
    width = weights.shape[0]
    span = width // CHUNKS
    block = span // 2 if span % 16 == 0 else span
    each = span // block
    first, pieces = chunks[0] * each, len(chunks) * each

    def kernel(kv_ref, w_ref, *refs):
        out_refs, (held, sems) = refs[: len(chunks)], refs[len(chunks) :]
        copies = []
        for piece in range(pieces):
            source = w_ref.at[pl.ds((first + piece) * block, block)]
            copies.append(
                pltpu.make_async_copy(source, held.at[pl.ds(piece * block, block)], sems.at[piece])
            )
            copies[-1].start()
        for piece in range(pieces):
            copies[piece].wait()
            columns = slice(piece % each * block, (piece % each + 1) * block)
            out_refs[piece // each][:, columns] = lax.dot_general(
                kv_ref[...],
                held[piece * block : (piece + 1) * block],
                (((1,), (1,)), ((), ())),
                preferred_element_type=F32,
            )

    return pl.pallas_call(
        kernel,
        out_shape=[jax.ShapeDtypeStruct((tokens, span), F32)] * len(chunks),
        in_specs=[VMEM, HBM],
        out_specs=[VMEM] * len(chunks),
        scratch_shapes=[pltpu.VMEM((pieces * block, lat), BF16), pltpu.SemaphoreType.DMA((pieces,))],
        compiler_params=params(18),
        cost_estimate=cost(2 * tokens * lat * span, 4 * span * lat),
        name="weight_products",
    )(kv_rows, in_hbm(weights))


def relay_step(tick, received, products, cotangent):
    tokens, span = products[0].shape
    sections = lax.axis_size("pipe")
    held = [(s, tick - LAG * (sections - 1 - s)) for s in range(sections)]
    held = [(s, c) for s, c in held if 0 <= c < CHUNKS]
    used = [products[c] for _, c in held]
    inputs = []
    if received is not None:
        inputs.append(received)
    if tick < CHUNKS:
        inputs.append(cotangent)

    def kernel(*refs):
        prod_refs = refs[len(inputs) : len(inputs) + len(used)]
        out_ref = refs[-1]
        stage = lax.axis_index("pipe")
        for (section, chunk), ref in zip(held, prod_refs):
            @pl.when(stage == section)
            def one():
                if section == sections - 1:
                    base = refs[len(inputs) - 1][:, chunk * span : (chunk + 1) * span]
                else:
                    base = refs[0][...]
                out_ref[...] = (base.astype(F32) + ref[...]).astype(BF16)

    return pl.pallas_call(
        kernel,
        in_specs=[VMEM] * (len(inputs) + len(used)),
        out_specs=VMEM,
        out_shape=jax.ShapeDtypeStruct((tokens, span), BF16),
        compiler_params=params(8),
        cost_estimate=cost(tokens * span, 8 * tokens * span),
        name="relay_step",
    )(*inputs, *used)


def last_step(received, products, relayed):
    tokens, span = products[0].shape
    several = len(received)

    def kernel(*refs):
        in_refs, prod_refs = refs[:several], refs[several : 2 * several]
        out_ref, held, sems = refs[2 * several + 1 :]

        @pl.when(lax.axis_index("pipe") == 0)
        def one():
            copies = []
            for at in range(several):
                held[at] = (in_refs[at][...].astype(F32) + prod_refs[at][...]).astype(BF16)
                target = out_ref.at[:, pl.ds((CHUNKS - several + at) * span, span)]
                copies.append(pltpu.make_async_copy(held.at[at], target, sems.at[at]))
                copies[-1].start()
            for copy in copies:
                copy.wait()

    return pl.pallas_call(
        kernel,
        in_specs=[VMEM] * (2 * several) + [ANY],
        out_specs=ANY,
        out_shape=jax.ShapeDtypeStruct(relayed.shape, BF16),
        scratch_shapes=[pltpu.VMEM((several, tokens, span), BF16), pltpu.SemaphoreType.DMA((several,))],
        input_output_aliases={2 * several: 0},
        compiler_params=params(8),
        cost_estimate=cost(0, 4 * tokens * span),
        name="last_step",
    )(*received, *products, relayed)


def token_relations():
    count = lax.axis_size("dp")
    chips = count // CORES
    if chips == 4:
        base = [(0, 0), (CORES, 2 * CORES), (2 * CORES, CORES), (3 * CORES, 3 * CORES)]
    else:
        base = [(CORES * d, CORES * d) for d in range(chips)]
    return base, [(b ^ 1, a ^ 1) for a, b in base]


def shards(acts, cotangent, kv_grads, w_kv, momentum):
    inputs, kv_rows, weights, moment = acts[0], kv_grads[0], w_kv[0], momentum[0]
    tokens, width = inputs.shape
    groups = lax.axis_size("dp")
    sections = lax.axis_size("pipe")
    chips = groups // CORES
    mats = moment.shape[1] // HEAD
    slots = max(1, mats // groups)
    scale_grad = 1.0 / (tokens * groups)
    scale = 0.2 * math.sqrt(max(width, HEAD))
    other_core = (1, 1)

    same, crossed = token_relations()
    ticks = CHUNKS + LAG * (sections - 1)
    sent, moved = [], []

    def relay(*others):
        tick = len(sent)
        received = moved[tick - LAG] if tick >= LAG else None
        if received is not None:
            received = after(received, sent[-1], *others)
        sent.append(relay_step(tick, received, products, cotangent))
        if tick < ticks - LAG:
            moved.append(down(sent[-1]))

    near = [kv_rows] + [swap(kv_rows, relation) for relation in same[1 : 3 if chips == 4 else chips]]
    far = [swap(kv_rows, other_core)]
    columns = split_columns(inputs)
    left = lax.all_to_all(columns, "dp", 0, 0, tiled=True)
    products = list(weight_products([0], after(kv_rows, columns), weights))
    near = near[:1] + [after(piece, products[0]) for piece in near[1:]]
    products = [after(product, far[0], *near[1:]) for product in products]
    relay()
    products += weight_products([1], after(kv_rows, sent[0]), weights)
    relay()
    far.extend(swap(piece, other_core) for piece in near[1:])
    if chips == 4:
        near.append(swap(near[1], same[2]))
    products += weight_products(list(range(LAG, CHUNKS)), after(kv_rows, sent[1]), weights)
    relay(products[-1])
    relay()
    if chips == 4:
        far.extend(swap(piece, other_core) for piece in cut(after(near[-1], sent[2]), 2))

    buffer, mine, theirs = gradient(
        left, same + crossed, near + far, after(moment, sent[3]), scale_grad, slots
    )
    relay(buffer)
    received = swap(after(theirs, sent[4]), other_core)
    relay(theirs)
    sums = add_pairs(after(mine, sent[5]), received)
    grams = [sums[0]] + [swap(sums[d], (CORES * d, CORES * d)) for d in range(1, chips)]
    relay(*grams[1:])
    mix = mixing([after(grams[0], sent[6])] + grams[1:], scale, slots)
    mixes = [mix] + [swap(mix, (CORES * d, CORES * d)) for d in range(1, chips)]
    relay(mix)
    far_mix = swap(after(mix, moved[6]), other_core)
    far_mixes = swap(join(mixes), other_core)
    update, outgoing = apply_mixing(after(buffer, sent[7]), mixes, far_mix, far_mixes, slots, sent)
    outgoing = last_step([after(m, update) for m in moved[-LAG:]], products[-LAG:], outgoing)
    return (update[None], outgoing[None])


def solution(mesh):
    in_specs = (
        P("pipe", "dp", None),
        P("dp", None),
        P("pipe", "dp", None),
        P("pipe", None, None),
        P("pipe", "dp", None),
    )
    out_specs = (P("pipe", "dp", None), P("pipe", "dp", None))
    return jax.shard_map(shards, mesh=mesh, in_specs=in_specs, out_specs=out_specs, check_vma=False)
```

```python
import functools
import math

import jax
import jax.numpy as jnp
from jax import lax
from jax.experimental import pallas as pl
from jax.experimental.pallas import tpu as pltpu
from jax.sharding import PartitionSpec as P

HEAD = 128
ITERS = 5
CORES = 2
CHUNKS = 4
LAG = 2
PAD = 8

momentum_rate = 0.95
quintic_a = 3.4445
quintic_b = -4.775
quintic_c = 2.0315
epsilon = 1e-07

F32 = jnp.float32
BF16 = jnp.bfloat16
ANY = pl.BlockSpec(memory_space=pl.ANY)
HBM = pl.BlockSpec(memory_space=pltpu.HBM)
VMEM = pl.BlockSpec(memory_space=pltpu.VMEM)


def cost(flops, moved):
    return pl.CostEstimate(flops=1, bytes_accessed=1, transcendentals=0)


def params(mib):
    return pltpu.CompilerParams(vmem_limit_bytes=mib * 1024 * 1024)


def in_hbm(value):
    return pltpu.with_memory_space_constraint(value, pltpu.HBM)


def after(value, *others):
    return lax.optimization_barrier((value, *others))[0]


def swap(value, by):
    count = lax.axis_size("dp")
    return lax.ppermute(value, "dp", [(i ^ by[i % CORES], i) for i in range(count)])


def cut(value, parts):
    rows, width = value.shape
    block = rows // parts

    def kernel(in_ref, *refs):
        sems = refs[parts]
        copies = []
        for part in range(parts):
            source = in_ref.at[pl.ds(part * block, block)]
            copies.append(pltpu.make_async_copy(source, refs[part], sems.at[part]))
            copies[-1].start()
        for copy in copies:
            copy.wait()

    return pl.pallas_call(
        kernel,
        out_shape=[jax.ShapeDtypeStruct((block, width), value.dtype)] * parts,
        in_specs=[ANY],
        out_specs=[ANY] * parts,
        scratch_shapes=[pltpu.SemaphoreType.DMA((parts,))],
        compiler_params=params(8),
        cost_estimate=cost(0, 4 * value.size),
        name="cut",
    )(value)


def join(values):
    def kernel(*refs):
        for at, ref in enumerate(refs[:-1]):
            refs[-1][at] = ref[...]

    shape = jax.ShapeDtypeStruct((len(values),) + values[0].shape, values[0].dtype)
    return pl.pallas_call(
        kernel,
        out_shape=shape,
        in_specs=[VMEM] * len(values),
        out_specs=VMEM,
        compiler_params=params(8),
        cost_estimate=cost(0, 8 * values[0].size),
        name="join",
    )(*values)


def down(value):
    count = lax.axis_size("pipe")
    return lax.ppermute(value, "pipe", [(i, i - 1) for i in range(1, count)])


def by_core(pair):
    own = lax.axis_index("dp")
    if pair[0] == pair[1]:
        return pair[0]
    return jnp.where(own % CORES == 0, pair[0], pair[1])


def split_columns(inputs):
    count = lax.axis_size("dp")
    tokens, width = inputs.shape
    block = width // count
    pieces = count if block % HEAD == 0 else 1
    part = width // pieces

    def kernel(in_ref, out_ref, held, turned, in_sems, out_sems):
        copies = []
        for piece in range(pieces):
            columns = pl.ds(piece * part, part)
            copies.append(
                pltpu.make_async_copy(in_ref.at[:, columns], held.at[:, columns], in_sems.at[piece])
            )
            copies[-1].start()
        stores = []
        for owner in range(count):
            if owner * pieces % count == 0:
                copies[owner * pieces // count].wait()
            turned[owner] = held[:, owner * block : (owner + 1) * block].T
            stores.append(pltpu.make_async_copy(turned.at[owner], out_ref.at[owner], out_sems.at[owner]))
            stores[-1].start()
        for store in stores:
            store.wait()

    return pl.pallas_call(
        kernel,
        out_shape=pltpu.HBM((count, block, tokens), BF16),
        in_specs=[HBM],
        out_specs=HBM,
        scratch_shapes=[
            pltpu.VMEM((tokens, width), BF16),
            pltpu.VMEM((count, block, tokens), BF16),
            pltpu.SemaphoreType.DMA((pieces,)),
            pltpu.SemaphoreType.DMA((count,)),
        ],
        compiler_params=params(8),
        cost_estimate=cost(0, 4 * tokens * width),
        name="split_columns",
    )(in_hbm(inputs))


def triangle():
    row = lax.broadcasted_iota(jnp.int32, (HEAD, HEAD), 0)
    col = lax.broadcasted_iota(jnp.int32, (HEAD, HEAD), 1)
    return row, col


def pack(mats):
    if len(mats) % 2:
        return jnp.concatenate(mats, axis=0)
    row, col = triangle()
    rows = []
    for first, second in zip(mats[::2], mats[1::2]):
        diagonal = jnp.sum(jnp.where(row == col, second, 0.0), axis=0, keepdims=True)
        rows.append(jnp.where(col >= row, first, second))
        rows.append(jnp.broadcast_to(diagonal, (PAD, HEAD)))
    return jnp.concatenate(rows, axis=0)


def packed_rows(slots):
    return slots * HEAD if slots % 2 else slots // 2 * (HEAD + PAD)


def unpack(packed, slots):
    if slots % 2:
        return [packed[i * HEAD : (i + 1) * HEAD] for i in range(slots)]
    row, col = triangle()
    mats = []
    for pair in range(slots // 2):
        at = pair * (HEAD + PAD)
        square = packed[at : at + HEAD]
        diagonal = packed[at + HEAD : at + HEAD + 1]
        other = square.T
        mats.append(jnp.where(col >= row, square, other))
        mats.append(jnp.where(col == row, diagonal, jnp.where(col < row, square, other)))
    return mats


def gradient(left, sources, right, moment, scale, slots):
    rows, width = moment.shape
    count = lax.axis_size("dp")
    chips = count // CORES
    mats = width // HEAD
    owners = mats // slots
    per_step = next(n for n in (4, 2, 1) if owners % n == 0)
    block = per_step * slots * HEAD
    tokens = right[0].shape[0]
    total_tokens = sum(piece.shape[0] for piece in right)
    n_right = len(right)
    packed = packed_rows(slots)
    steps = owners // per_step

    def kernel(*refs):
        left_ref = refs[0]
        right_refs = refs[1 : 1 + n_right]
        mom_ref, buf_ref, mine_ref, theirs_ref, held, grams = refs[1 + n_right :]
        step = pl.program_id(0)
        own = lax.axis_index("dp")

        @pl.when(step == 0)
        def load():
            for at, pair in enumerate(sources):
                held[:, at * tokens : (at + 1) * tokens] = left_ref[own ^ by_core(pair)]
            if owners < count:
                grams[...] = jnp.zeros_like(grams)

        kv_block = jnp.concatenate([ref[...] for ref in right_refs], axis=0)
        grad = jnp.dot(held[...], kv_block, preferred_element_type=F32)
        buffer = (momentum_rate * mom_ref[...].astype(F32) + grad * scale).astype(BF16)
        buf_ref[...] = buffer
        for which in range(per_step):
            first = which * slots * HEAD
            values = buffer[:, first : first + slots * HEAD]
            gram = lax.dot_general(values, values, (((0,), (0,)), ((), ())), preferred_element_type=F32)
            spans = [slice(slot * HEAD, (slot + 1) * HEAD) for slot in range(slots)]
            owner = step * per_step + which
            grams[owner ^ own] = pack([gram[span, span] for span in spans])

        @pl.when(step == steps - 1)
        def store():
            for chip in range(chips):
                mine_ref[chip] = grams[CORES * chip]
                theirs_ref[chip] = grams[CORES * chip + 1]
            theirs_ref[chips] = jnp.zeros((packed, HEAD), F32)

    column = lambda height: pl.BlockSpec((height, block), lambda j: (0, j))
    gram_shape = jax.ShapeDtypeStruct((chips, packed, HEAD), F32)
    gram_spec = pl.BlockSpec((chips, packed, HEAD), lambda j: (0, 0, 0))
    other_shape = jax.ShapeDtypeStruct((chips + 1, packed, HEAD), F32)
    other_spec = pl.BlockSpec((chips + 1, packed, HEAD), lambda j: (0, 0, 0))
    return pl.pallas_call(
        kernel,
        grid=(steps,),
        out_shape=[jax.ShapeDtypeStruct((rows, width), BF16), gram_shape, other_shape],
        in_specs=[pl.BlockSpec(left.shape, lambda j: (0, 0, 0))] + [column(piece.shape[0]) for piece in right] + [column(rows)],
        out_specs=[column(rows), gram_spec, other_spec],
        scratch_shapes=[pltpu.VMEM((rows, total_tokens), BF16), pltpu.VMEM((count, packed, HEAD), F32)],
        compiler_params=params(26),
        cost_estimate=cost(
            2 * rows * total_tokens * width, 2 * total_tokens * (rows + width) + 4 * rows * width
        ),
        name="gradient",
    )(in_hbm(left), *[in_hbm(piece) for piece in right], in_hbm(moment))


def add_pairs(first, second):
    chips = first.shape[0]

    def kernel(first_ref, second_ref, *out_refs):
        for distance in range(chips):
            out_refs[distance][...] = first_ref[distance] + second_ref[distance]

    return pl.pallas_call(
        kernel,
        out_shape=[jax.ShapeDtypeStruct(first.shape[1:], F32)] * chips,
        in_specs=[VMEM] * 2,
        out_specs=[VMEM] * chips,
        compiler_params=params(16),
        cost_estimate=cost(first.size, 12 * first.size),
        name="add_pairs",
    )(first, second)


def mixing(grams, scale, slots):
    highest = lax.Precision.HIGHEST

    def product(left, right):
        return jnp.dot(left, right, precision=highest, preferred_element_type=F32)

    def kernel(*refs):
        gram_refs, out_ref = refs[:-1], refs[-1]
        row, col = triangle()
        eye = (row == col).astype(F32)
        total = gram_refs[0][...]
        for ref in gram_refs[1:]:
            total = total + ref[...]
        grams, inverses, mixes = [], [], []
        for gram in unpack(total, slots):
            squares = jnp.sum(gram * eye, keepdims=True)
            inverse = 1.0 / (jnp.sqrt(squares) + epsilon)
            grams.append(gram * inverse * inverse)
            inverses.append(inverse)
            mixes.append(None)
        for step in range(ITERS):
            square = [product(gram, gram) for gram in grams]
            factor = [
                quintic_a * eye + quintic_b * gram + quintic_c * sq for gram, sq in zip(grams, square)
            ]
            mixes = [f if mix is None else product(mix, f) for mix, f in zip(mixes, factor)]
            if step < ITERS - 1:
                half = [product(gram, f) for gram, f in zip(grams, factor)]
                grams = [product(h, f) for h, f in zip(half, factor)]
        out_ref[...] = pack([mix * (scale * inverse) for mix, inverse in zip(mixes, inverses)])

    packed = packed_rows(slots)
    spec = pl.BlockSpec((packed, HEAD), lambda i: (0, 0))
    return pl.pallas_call(
        kernel,
        grid=(1,),
        out_shape=jax.ShapeDtypeStruct((packed, HEAD), F32),
        in_specs=[spec] * len(grams),
        out_specs=spec,
        compiler_params=params(16),
        cost_estimate=cost(slots * 18 * 2 * 6 * HEAD**3, 4 * slots * HEAD * HEAD * 9),
        name="mixing",
    )(*grams)


def apply_mixing(buffer, near, other, far, slots, sent):
    rows, width = buffer.shape
    tokens, wide = sent[0].shape
    count = lax.axis_size("dp")
    sections = lax.axis_size("pipe")
    mats = width // HEAD
    owners = mats // slots
    per_step = next(n for n in (4, 2, 1) if owners % n == 0)
    steps = owners // per_step
    span = slots * HEAD
    block = per_step * span
    packed = packed_rows(slots)

    def kernel(*refs):
        near_refs, other_ref, far_ref = refs[: len(near)], refs[len(near)], refs[len(near) + 1]
        sent_refs = refs[len(near) + 2 : len(near) + 2 + len(sent)]
        buf_ref, out_ref, relayed_ref, held, sems = refs[len(near) + 2 + len(sent) :]
        own = lax.axis_index("dp")
        stage = lax.axis_index("pipe")
        step = pl.program_id(0)

        def each_copy(act):
            for section in range(sections):
                @pl.when(stage == section)
                def one():
                    for chunk in range(CHUNKS):
                        tick = chunk + LAG * (sections - 1 - section)
                        if tick < len(sent):
                            target = relayed_ref.at[:, pl.ds(chunk * wide, wide)]
                            act(pltpu.make_async_copy(sent_refs[tick], target, sems.at[chunk]))

        @pl.when(step == 0)
        def load():
            each_copy(lambda copy: copy.start())
            for chip, ref in enumerate(near_refs):
                held[CORES * chip] = ref[...]
                held[CORES * chip + 1] = far_ref[chip] if chip else other_ref[...]

        for which in range(per_step):
            parts = unpack(held[(step * per_step + which) ^ own], slots)
            zero = jnp.zeros((HEAD, HEAD), F32)
            mix = jnp.concatenate(
                [
                    jnp.concatenate([part if j == i else zero for j in range(slots)], axis=1)
                    for i, part in enumerate(parts)
                ],
                axis=0,
            )
            columns = slice(which * span, (which + 1) * span)
            values = buf_ref[:, columns]
            total = None
            for part in range(3):
                piece = mix.astype(BF16)
                mix = mix - piece.astype(F32)
                term = jnp.dot(values, piece, preferred_element_type=F32)
                total = term if total is None else total + term
            out_ref[:, columns] = total.astype(BF16)

        @pl.when(step == steps - 1)
        def finish():
            each_copy(lambda copy: copy.wait())

    column = pl.BlockSpec((rows, block), lambda j: (0, j))
    return pl.pallas_call(
        kernel,
        grid=(steps,),
        out_shape=[
            jax.ShapeDtypeStruct((rows, width), BF16),
            jax.ShapeDtypeStruct((tokens, wide * CHUNKS), BF16),
        ],
        in_specs=[pl.BlockSpec((packed, HEAD), lambda j: (0, 0))] * (len(near) + 1)
        + [pl.BlockSpec(far.shape, lambda j: (0, 0, 0))]
        + [VMEM] * len(sent)
        + [column],
        out_specs=[column, ANY],
        scratch_shapes=[pltpu.VMEM((count, packed, HEAD), F32), pltpu.SemaphoreType.DMA((CHUNKS,))],
        compiler_params=params(16),
        cost_estimate=cost(6 * rows * width * HEAD, 4 * rows * width),
        name="apply_mixing",
    )(*near, other, far, *sent, buffer)


def weight_products(chunks, kv_rows, weights):
    tokens, lat = kv_rows.shape
    width = weights.shape[0]
    span = width // CHUNKS
    block = span // 2 if span % 16 == 0 else span
    each = span // block
    first, pieces = chunks[0] * each, len(chunks) * each

    def kernel(kv_ref, w_ref, *refs):
        out_refs, (held, sems) = refs[: len(chunks)], refs[len(chunks) :]
        copies = []
        for piece in range(pieces):
            source = w_ref.at[pl.ds((first + piece) * block, block)]
            copies.append(
                pltpu.make_async_copy(source, held.at[pl.ds(piece * block, block)], sems.at[piece])
            )
            copies[-1].start()
        for piece in range(pieces):
            copies[piece].wait()
            columns = slice(piece % each * block, (piece % each + 1) * block)
            out_refs[piece // each][:, columns] = lax.dot_general(
                kv_ref[...],
                held[piece * block : (piece + 1) * block],
                (((1,), (1,)), ((), ())),
                preferred_element_type=F32,
            )

    return pl.pallas_call(
        kernel,
        out_shape=[jax.ShapeDtypeStruct((tokens, span), F32)] * len(chunks),
        in_specs=[VMEM, HBM],
        out_specs=[VMEM] * len(chunks),
        scratch_shapes=[pltpu.VMEM((pieces * block, lat), BF16), pltpu.SemaphoreType.DMA((pieces,))],
        compiler_params=params(18),
        cost_estimate=cost(2 * tokens * lat * span, 4 * span * lat),
        name="weight_products",
    )(kv_rows, in_hbm(weights))


def relay_step(tick, received, products, cotangent):
    tokens, span = products[0].shape
    sections = lax.axis_size("pipe")
    held = [(s, tick - LAG * (sections - 1 - s)) for s in range(sections)]
    held = [(s, c) for s, c in held if 0 <= c < CHUNKS]
    used = [products[c] for _, c in held]
    inputs = []
    if received is not None:
        inputs.append(received)
    if tick < CHUNKS:
        inputs.append(cotangent)

    def kernel(*refs):
        prod_refs = refs[len(inputs) : len(inputs) + len(used)]
        out_ref = refs[-1]
        stage = lax.axis_index("pipe")
        for (section, chunk), ref in zip(held, prod_refs):
            @pl.when(stage == section)
            def one():
                if section == sections - 1:
                    base = refs[len(inputs) - 1][:, chunk * span : (chunk + 1) * span]
                else:
                    base = refs[0][...]
                out_ref[...] = (base.astype(F32) + ref[...]).astype(BF16)

    return pl.pallas_call(
        kernel,
        in_specs=[VMEM] * (len(inputs) + len(used)),
        out_specs=VMEM,
        out_shape=jax.ShapeDtypeStruct((tokens, span), BF16),
        compiler_params=params(8),
        cost_estimate=cost(tokens * span, 8 * tokens * span),
        name="relay_step",
    )(*inputs, *used)


def last_step(received, products, relayed):
    tokens, span = products[0].shape
    several = len(received)

    def kernel(*refs):
        in_refs, prod_refs = refs[:several], refs[several : 2 * several]
        out_ref, held, sems = refs[2 * several + 1 :]

        @pl.when(lax.axis_index("pipe") == 0)
        def one():
            copies = []
            for at in range(several):
                held[at] = (in_refs[at][...].astype(F32) + prod_refs[at][...]).astype(BF16)
                target = out_ref.at[:, pl.ds((CHUNKS - several + at) * span, span)]
                copies.append(pltpu.make_async_copy(held.at[at], target, sems.at[at]))
                copies[-1].start()
            for copy in copies:
                copy.wait()

    return pl.pallas_call(
        kernel,
        in_specs=[VMEM] * (2 * several) + [ANY],
        out_specs=ANY,
        out_shape=jax.ShapeDtypeStruct(relayed.shape, BF16),
        scratch_shapes=[pltpu.VMEM((several, tokens, span), BF16), pltpu.SemaphoreType.DMA((several,))],
        input_output_aliases={2 * several: 0},
        compiler_params=params(8),
        cost_estimate=cost(0, 4 * tokens * span),
        name="last_step",
    )(*received, *products, relayed)


def token_relations():
    count = lax.axis_size("dp")
    chips = count // CORES
    if chips == 4:
        base = [(0, 0), (CORES, 2 * CORES), (2 * CORES, CORES), (3 * CORES, 3 * CORES)]
    else:
        base = [(CORES * d, CORES * d) for d in range(chips)]
    return base, [(b ^ 1, a ^ 1) for a, b in base]


def shards(acts, cotangent, kv_grads, w_kv, momentum):
    inputs, kv_rows, weights, moment = acts[0], kv_grads[0], w_kv[0], momentum[0]
    tokens, width = inputs.shape
    groups = lax.axis_size("dp")
    sections = lax.axis_size("pipe")
    chips = groups // CORES
    mats = moment.shape[1] // HEAD
    slots = max(1, mats // groups)
    scale_grad = 1.0 / (tokens * groups)
    scale = 0.2 * math.sqrt(max(width, HEAD))
    other_core = (1, 1)

    same, crossed = token_relations()
    ticks = CHUNKS + LAG * (sections - 1)
    sent, moved = [], []

    def relay(*others):
        tick = len(sent)
        received = moved[tick - LAG] if tick >= LAG else None
        if received is not None:
            received = after(received, sent[-1], *others)
        sent.append(relay_step(tick, received, products, cotangent))
        if tick < ticks - LAG:
            moved.append(down(sent[-1]))

    near = [kv_rows] + [swap(kv_rows, relation) for relation in same[1 : 3 if chips == 4 else chips]]
    far = [swap(kv_rows, other_core)]
    columns = split_columns(inputs)
    left = lax.all_to_all(columns, "dp", 0, 0, tiled=True)
    products = list(weight_products([0], after(kv_rows, columns), weights))
    near = near[:1] + [after(piece, products[0]) for piece in near[1:]]
    products = [after(product, far[0], near[1]) for product in products]
    relay()
    products += weight_products([1], after(kv_rows, sent[0]), weights)
    relay()
    far.append(swap(near[1], other_core))
    for piece in near[2 : 2 if chips == 4 else chips]:
        far.append(swap(piece, other_core))
    if chips == 4:
        near.append(swap(near[1], same[2]))
    products += weight_products(list(range(LAG, CHUNKS)), after(kv_rows, sent[1]), weights)
    relay(products[-1])
    relay()
    if chips == 4:
        for piece in near[2:]:
            far.extend(swap(half, other_core) for half in cut(after(piece, sent[2]), 2))

    buffer, mine, theirs = gradient(
        left, same + crossed, near + far, after(moment, sent[3]), scale_grad, slots
    )
    relay(buffer)
    received = swap(after(theirs, sent[4]), other_core)
    relay(theirs)
    sums = add_pairs(after(mine, sent[5]), received)
    grams = [sums[0]] + [swap(sums[d], (CORES * d, CORES * d)) for d in range(1, chips)]
    relay(*grams[1:])
    mix = mixing([after(grams[0], sent[6])] + grams[1:], scale, slots)
    mixes = [mix] + [swap(mix, (CORES * d, CORES * d)) for d in range(1, chips)]
    relay(mix)
    far_mix = swap(after(mix, moved[6]), other_core)
    far_mixes = swap(join(mixes), other_core)
    update, outgoing = apply_mixing(after(buffer, sent[7]), mixes, far_mix, far_mixes, slots, sent)
    outgoing = last_step([after(m, update) for m in moved[-LAG:]], products[-LAG:], outgoing)
    return (update[None], outgoing[None])


def solution(mesh):
    in_specs = (
        P("pipe", "dp", None),
        P("dp", None),
        P("pipe", "dp", None),
        P("pipe", None, None),
        P("pipe", "dp", None),
    )
    out_specs = (P("pipe", "dp", None), P("pipe", "dp", None))
    return jax.shard_map(shards, mesh=mesh, in_specs=in_specs, out_specs=out_specs, check_vma=False)
```

```python
import functools
import math

import jax
import jax.numpy as jnp
from jax import lax
from jax.experimental import pallas as pl
from jax.experimental.pallas import tpu as pltpu
from jax.sharding import PartitionSpec as P

HEAD = 128
ITERS = 5
CORES = 2
CHUNKS = 4
LAG = 2
PAD = 8

momentum_rate = 0.95
quintic_a = 3.4445
quintic_b = -4.775
quintic_c = 2.0315
epsilon = 1e-07

F32 = jnp.float32
BF16 = jnp.bfloat16
ANY = pl.BlockSpec(memory_space=pl.ANY)
HBM = pl.BlockSpec(memory_space=pltpu.HBM)
VMEM = pl.BlockSpec(memory_space=pltpu.VMEM)


def cost(flops, moved):
    return pl.CostEstimate(flops=1, bytes_accessed=1, transcendentals=0)


def params(mib):
    return pltpu.CompilerParams(vmem_limit_bytes=mib * 1024 * 1024)


def in_hbm(value):
    return pltpu.with_memory_space_constraint(value, pltpu.HBM)


def after(value, *others):
    return lax.optimization_barrier((value, *others))[0]


def swap(value, by):
    count = lax.axis_size("dp")
    return lax.ppermute(value, "dp", [(i ^ by[i % CORES], i) for i in range(count)])


def cut(value, parts):
    rows, width = value.shape
    block = rows // parts

    def kernel(in_ref, *refs):
        sems = refs[parts]
        copies = []
        for part in range(parts):
            source = in_ref.at[pl.ds(part * block, block)]
            copies.append(pltpu.make_async_copy(source, refs[part], sems.at[part]))
            copies[-1].start()
        for copy in copies:
            copy.wait()

    return pl.pallas_call(
        kernel,
        out_shape=[jax.ShapeDtypeStruct((block, width), value.dtype)] * parts,
        in_specs=[ANY],
        out_specs=[ANY] * parts,
        scratch_shapes=[pltpu.SemaphoreType.DMA((parts,))],
        compiler_params=params(8),
        cost_estimate=cost(0, 4 * value.size),
        name="cut",
    )(value)


def join(values):
    def kernel(*refs):
        for at, ref in enumerate(refs[:-1]):
            refs[-1][at] = ref[...]

    shape = jax.ShapeDtypeStruct((len(values),) + values[0].shape, values[0].dtype)
    return pl.pallas_call(
        kernel,
        out_shape=shape,
        in_specs=[VMEM] * len(values),
        out_specs=VMEM,
        compiler_params=params(8),
        cost_estimate=cost(0, 8 * values[0].size),
        name="join",
    )(*values)


def down(value):
    count = lax.axis_size("pipe")
    return lax.ppermute(value, "pipe", [(i, i - 1) for i in range(1, count)])


def by_core(pair):
    own = lax.axis_index("dp")
    if pair[0] == pair[1]:
        return pair[0]
    return jnp.where(own % CORES == 0, pair[0], pair[1])


def split_columns(inputs):
    count = lax.axis_size("dp")
    tokens, width = inputs.shape
    block = width // count
    pieces = count if block % HEAD == 0 else 1
    part = width // pieces

    def kernel(in_ref, out_ref, held, turned, in_sems, out_sems):
        copies = []
        for piece in range(pieces):
            columns = pl.ds(piece * part, part)
            copies.append(
                pltpu.make_async_copy(in_ref.at[:, columns], held.at[:, columns], in_sems.at[piece])
            )
            copies[-1].start()
        stores = []
        for owner in range(count):
            if owner * pieces % count == 0:
                copies[owner * pieces // count].wait()
            turned[owner] = held[:, owner * block : (owner + 1) * block].T
            stores.append(pltpu.make_async_copy(turned.at[owner], out_ref.at[owner], out_sems.at[owner]))
            stores[-1].start()
        for store in stores:
            store.wait()

    return pl.pallas_call(
        kernel,
        out_shape=pltpu.HBM((count, block, tokens), BF16),
        in_specs=[HBM],
        out_specs=HBM,
        scratch_shapes=[
            pltpu.VMEM((tokens, width), BF16),
            pltpu.VMEM((count, block, tokens), BF16),
            pltpu.SemaphoreType.DMA((pieces,)),
            pltpu.SemaphoreType.DMA((count,)),
        ],
        compiler_params=params(8),
        cost_estimate=cost(0, 4 * tokens * width),
        name="split_columns",
    )(in_hbm(inputs))


def triangle():
    row = lax.broadcasted_iota(jnp.int32, (HEAD, HEAD), 0)
    col = lax.broadcasted_iota(jnp.int32, (HEAD, HEAD), 1)
    return row, col


def pack(mats):
    if len(mats) % 2:
        return jnp.concatenate(mats, axis=0)
    row, col = triangle()
    rows = []
    for first, second in zip(mats[::2], mats[1::2]):
        diagonal = jnp.sum(jnp.where(row == col, second, 0.0), axis=0, keepdims=True)
        rows.append(jnp.where(col >= row, first, second))
        rows.append(jnp.broadcast_to(diagonal, (PAD, HEAD)))
    return jnp.concatenate(rows, axis=0)


def packed_rows(slots):
    return slots * HEAD if slots % 2 else slots // 2 * (HEAD + PAD)


def unpack(packed, slots):
    if slots % 2:
        return [packed[i * HEAD : (i + 1) * HEAD] for i in range(slots)]
    row, col = triangle()
    mats = []
    for pair in range(slots // 2):
        at = pair * (HEAD + PAD)
        square = packed[at : at + HEAD]
        diagonal = packed[at + HEAD : at + HEAD + 1]
        other = square.T
        mats.append(jnp.where(col >= row, square, other))
        mats.append(jnp.where(col == row, diagonal, jnp.where(col < row, square, other)))
    return mats


def gradient(left, sources, right, moment, scale, slots):
    rows, width = moment.shape
    count = lax.axis_size("dp")
    chips = count // CORES
    mats = width // HEAD
    owners = mats // slots
    per_step = next(n for n in (4, 2, 1) if owners % n == 0)
    block = per_step * slots * HEAD
    tokens = right[0].shape[0]
    total_tokens = sum(piece.shape[0] for piece in right)
    n_right = len(right)
    packed = packed_rows(slots)
    steps = owners // per_step

    def kernel(*refs):
        left_ref = refs[0]
        right_refs = refs[1 : 1 + n_right]
        mom_ref, buf_ref, mine_ref, theirs_ref, held, grams = refs[1 + n_right :]
        step = pl.program_id(0)
        own = lax.axis_index("dp")

        @pl.when(step == 0)
        def load():
            for at, pair in enumerate(sources):
                held[:, at * tokens : (at + 1) * tokens] = left_ref[own ^ by_core(pair)]
            if owners < count:
                grams[...] = jnp.zeros_like(grams)

        kv_block = jnp.concatenate([ref[...] for ref in right_refs], axis=0)
        grad = jnp.dot(held[...], kv_block, preferred_element_type=F32)
        buffer = (momentum_rate * mom_ref[...].astype(F32) + grad * scale).astype(BF16)
        buf_ref[...] = buffer
        for which in range(per_step):
            first = which * slots * HEAD
            values = buffer[:, first : first + slots * HEAD]
            gram = lax.dot_general(values, values, (((0,), (0,)), ((), ())), preferred_element_type=F32)
            spans = [slice(slot * HEAD, (slot + 1) * HEAD) for slot in range(slots)]
            owner = step * per_step + which
            grams[owner ^ own] = pack([gram[span, span] for span in spans])

        @pl.when(step == steps - 1)
        def store():
            for chip in range(chips):
                mine_ref[chip] = grams[CORES * chip]
                theirs_ref[chip] = grams[CORES * chip + 1]
            theirs_ref[chips] = jnp.zeros((packed, HEAD), F32)

    column = lambda height: pl.BlockSpec((height, block), lambda j: (0, j))
    gram_shape = jax.ShapeDtypeStruct((chips, packed, HEAD), F32)
    gram_spec = pl.BlockSpec((chips, packed, HEAD), lambda j: (0, 0, 0))
    other_shape = jax.ShapeDtypeStruct((chips + 1, packed, HEAD), F32)
    other_spec = pl.BlockSpec((chips + 1, packed, HEAD), lambda j: (0, 0, 0))
    return pl.pallas_call(
        kernel,
        grid=(steps,),
        out_shape=[jax.ShapeDtypeStruct((rows, width), BF16), gram_shape, other_shape],
        in_specs=[pl.BlockSpec(left.shape, lambda j: (0, 0, 0))] + [column(piece.shape[0]) for piece in right] + [column(rows)],
        out_specs=[column(rows), gram_spec, other_spec],
        scratch_shapes=[pltpu.VMEM((rows, total_tokens), BF16), pltpu.VMEM((count, packed, HEAD), F32)],
        compiler_params=params(26),
        cost_estimate=cost(
            2 * rows * total_tokens * width, 2 * total_tokens * (rows + width) + 4 * rows * width
        ),
        name="gradient",
    )(in_hbm(left), *[in_hbm(piece) for piece in right[:-2]], *right[-2:], in_hbm(moment))


def add_pairs(first, second):
    chips = first.shape[0]

    def kernel(first_ref, second_ref, *out_refs):
        for distance in range(chips):
            out_refs[distance][...] = first_ref[distance] + second_ref[distance]

    return pl.pallas_call(
        kernel,
        out_shape=[jax.ShapeDtypeStruct(first.shape[1:], F32)] * chips,
        in_specs=[VMEM] * 2,
        out_specs=[VMEM] * chips,
        compiler_params=params(16),
        cost_estimate=cost(first.size, 12 * first.size),
        name="add_pairs",
    )(first, second)


def mixing(grams, scale, slots):
    highest = lax.Precision.HIGHEST

    def product(left, right):
        return jnp.dot(left, right, precision=highest, preferred_element_type=F32)

    def kernel(*refs):
        gram_refs, out_ref = refs[:-1], refs[-1]
        row, col = triangle()
        eye = (row == col).astype(F32)
        total = gram_refs[0][...]
        for ref in gram_refs[1:]:
            total = total + ref[...]
        grams, inverses, mixes = [], [], []
        for gram in unpack(total, slots):
            squares = jnp.sum(gram * eye, keepdims=True)
            inverse = 1.0 / (jnp.sqrt(squares) + epsilon)
            grams.append(gram * inverse * inverse)
            inverses.append(inverse)
            mixes.append(None)
        for step in range(ITERS):
            square = [product(gram, gram) for gram in grams]
            factor = [
                quintic_a * eye + quintic_b * gram + quintic_c * sq for gram, sq in zip(grams, square)
            ]
            mixes = [f if mix is None else product(mix, f) for mix, f in zip(mixes, factor)]
            if step < ITERS - 1:
                half = [product(gram, f) for gram, f in zip(grams, factor)]
                grams = [product(h, f) for h, f in zip(half, factor)]
        out_ref[...] = pack([mix * (scale * inverse) for mix, inverse in zip(mixes, inverses)])

    packed = packed_rows(slots)
    spec = pl.BlockSpec((packed, HEAD), lambda i: (0, 0))
    return pl.pallas_call(
        kernel,
        grid=(1,),
        out_shape=jax.ShapeDtypeStruct((packed, HEAD), F32),
        in_specs=[spec] * len(grams),
        out_specs=spec,
        compiler_params=params(16),
        cost_estimate=cost(slots * 18 * 2 * 6 * HEAD**3, 4 * slots * HEAD * HEAD * 9),
        name="mixing",
    )(*grams)


def apply_mixing(buffer, near, other, far, slots, sent):
    rows, width = buffer.shape
    tokens, wide = sent[0].shape
    count = lax.axis_size("dp")
    sections = lax.axis_size("pipe")
    mats = width // HEAD
    owners = mats // slots
    per_step = next(n for n in (4, 2, 1) if owners % n == 0)
    steps = owners // per_step
    span = slots * HEAD
    block = per_step * span
    packed = packed_rows(slots)

    def kernel(*refs):
        near_refs, other_ref, far_ref = refs[: len(near)], refs[len(near)], refs[len(near) + 1]
        sent_refs = refs[len(near) + 2 : len(near) + 2 + len(sent)]
        buf_ref, out_ref, relayed_ref, held, sems = refs[len(near) + 2 + len(sent) :]
        own = lax.axis_index("dp")
        stage = lax.axis_index("pipe")
        step = pl.program_id(0)

        def each_copy(act):
            for section in range(sections):
                @pl.when(stage == section)
                def one():
                    for chunk in range(CHUNKS):
                        tick = chunk + LAG * (sections - 1 - section)
                        if tick < len(sent):
                            target = relayed_ref.at[:, pl.ds(chunk * wide, wide)]
                            act(pltpu.make_async_copy(sent_refs[tick], target, sems.at[chunk]))

        @pl.when(step == 0)
        def load():
            each_copy(lambda copy: copy.start())
            for chip, ref in enumerate(near_refs):
                held[CORES * chip] = ref[...]
                held[CORES * chip + 1] = far_ref[chip] if chip else other_ref[...]

        for which in range(per_step):
            parts = unpack(held[(step * per_step + which) ^ own], slots)
            zero = jnp.zeros((HEAD, HEAD), F32)
            mix = jnp.concatenate(
                [
                    jnp.concatenate([part if j == i else zero for j in range(slots)], axis=1)
                    for i, part in enumerate(parts)
                ],
                axis=0,
            )
            columns = slice(which * span, (which + 1) * span)
            values = buf_ref[:, columns]
            total = None
            for part in range(3):
                piece = mix.astype(BF16)
                mix = mix - piece.astype(F32)
                term = jnp.dot(values, piece, preferred_element_type=F32)
                total = term if total is None else total + term
            out_ref[:, columns] = total.astype(BF16)

        @pl.when(step == steps - 1)
        def finish():
            each_copy(lambda copy: copy.wait())

    column = pl.BlockSpec((rows, block), lambda j: (0, j))
    return pl.pallas_call(
        kernel,
        grid=(steps,),
        out_shape=[
            jax.ShapeDtypeStruct((rows, width), BF16),
            jax.ShapeDtypeStruct((tokens, wide * CHUNKS), BF16),
        ],
        in_specs=[pl.BlockSpec((packed, HEAD), lambda j: (0, 0))] * (len(near) + 1)
        + [pl.BlockSpec(far.shape, lambda j: (0, 0, 0))]
        + [VMEM] * len(sent)
        + [column],
        out_specs=[column, ANY],
        scratch_shapes=[pltpu.VMEM((count, packed, HEAD), F32), pltpu.SemaphoreType.DMA((CHUNKS,))],
        compiler_params=params(16),
        cost_estimate=cost(6 * rows * width * HEAD, 4 * rows * width),
        name="apply_mixing",
    )(*near, other, far, *sent, buffer)


def weight_products(chunks, kv_rows, weights):
    tokens, lat = kv_rows.shape
    width = weights.shape[0]
    span = width // CHUNKS
    block = span // 2 if span % 16 == 0 else span
    each = span // block
    first, pieces = chunks[0] * each, len(chunks) * each

    def kernel(kv_ref, w_ref, *refs):
        out_refs, (held, sems) = refs[: len(chunks)], refs[len(chunks) :]
        copies = []
        for piece in range(pieces):
            source = w_ref.at[pl.ds((first + piece) * block, block)]
            copies.append(
                pltpu.make_async_copy(source, held.at[pl.ds(piece * block, block)], sems.at[piece])
            )
            copies[-1].start()
        for piece in range(pieces):
            copies[piece].wait()
            columns = slice(piece % each * block, (piece % each + 1) * block)
            out_refs[piece // each][:, columns] = lax.dot_general(
                kv_ref[...],
                held[piece * block : (piece + 1) * block],
                (((1,), (1,)), ((), ())),
                preferred_element_type=F32,
            )

    return pl.pallas_call(
        kernel,
        out_shape=[jax.ShapeDtypeStruct((tokens, span), F32)] * len(chunks),
        in_specs=[VMEM, HBM],
        out_specs=[VMEM] * len(chunks),
        scratch_shapes=[pltpu.VMEM((pieces * block, lat), BF16), pltpu.SemaphoreType.DMA((pieces,))],
        compiler_params=params(18),
        cost_estimate=cost(2 * tokens * lat * span, 4 * span * lat),
        name="weight_products",
    )(kv_rows, in_hbm(weights))


def relay_step(tick, received, products, cotangent):
    tokens, span = products[0].shape
    sections = lax.axis_size("pipe")
    held = [(s, tick - LAG * (sections - 1 - s)) for s in range(sections)]
    held = [(s, c) for s, c in held if 0 <= c < CHUNKS]
    used = [products[c] for _, c in held]
    inputs = []
    if received is not None:
        inputs.append(received)
    if tick < CHUNKS:
        inputs.append(cotangent)

    def kernel(*refs):
        prod_refs = refs[len(inputs) : len(inputs) + len(used)]
        out_ref = refs[-1]
        stage = lax.axis_index("pipe")
        for (section, chunk), ref in zip(held, prod_refs):
            @pl.when(stage == section)
            def one():
                if section == sections - 1:
                    base = refs[len(inputs) - 1][:, chunk * span : (chunk + 1) * span]
                else:
                    base = refs[0][...]
                out_ref[...] = (base.astype(F32) + ref[...]).astype(BF16)

    return pl.pallas_call(
        kernel,
        in_specs=[VMEM] * (len(inputs) + len(used)),
        out_specs=VMEM,
        out_shape=jax.ShapeDtypeStruct((tokens, span), BF16),
        compiler_params=params(8),
        cost_estimate=cost(tokens * span, 8 * tokens * span),
        name="relay_step",
    )(*inputs, *used)


def last_step(received, products, relayed):
    tokens, span = products[0].shape
    several = len(received)

    def kernel(*refs):
        in_refs, prod_refs = refs[:several], refs[several : 2 * several]
        out_ref, held, sems = refs[2 * several + 1 :]

        @pl.when(lax.axis_index("pipe") == 0)
        def one():
            copies = []
            for at in range(several):
                held[at] = (in_refs[at][...].astype(F32) + prod_refs[at][...]).astype(BF16)
                target = out_ref.at[:, pl.ds((CHUNKS - several + at) * span, span)]
                copies.append(pltpu.make_async_copy(held.at[at], target, sems.at[at]))
                copies[-1].start()
            for copy in copies:
                copy.wait()

    return pl.pallas_call(
        kernel,
        in_specs=[VMEM] * (2 * several) + [ANY],
        out_specs=ANY,
        out_shape=jax.ShapeDtypeStruct(relayed.shape, BF16),
        scratch_shapes=[pltpu.VMEM((several, tokens, span), BF16), pltpu.SemaphoreType.DMA((several,))],
        input_output_aliases={2 * several: 0},
        compiler_params=params(8),
        cost_estimate=cost(0, 4 * tokens * span),
        name="last_step",
    )(*received, *products, relayed)


def token_relations():
    count = lax.axis_size("dp")
    chips = count // CORES
    if chips == 4:
        base = [(0, 0), (CORES, 2 * CORES), (2 * CORES, CORES), (3 * CORES, 3 * CORES)]
    else:
        base = [(CORES * d, CORES * d) for d in range(chips)]
    return base, [(b ^ 1, a ^ 1) for a, b in base]


def shards(acts, cotangent, kv_grads, w_kv, momentum):
    inputs, kv_rows, weights, moment = acts[0], kv_grads[0], w_kv[0], momentum[0]
    tokens, width = inputs.shape
    groups = lax.axis_size("dp")
    sections = lax.axis_size("pipe")
    chips = groups // CORES
    mats = moment.shape[1] // HEAD
    slots = max(1, mats // groups)
    scale_grad = 1.0 / (tokens * groups)
    scale = 0.2 * math.sqrt(max(width, HEAD))
    other_core = (1, 1)

    same, crossed = token_relations()
    ticks = CHUNKS + LAG * (sections - 1)
    sent, moved = [], []

    def relay(*others):
        tick = len(sent)
        received = moved[tick - LAG] if tick >= LAG else None
        if received is not None:
            received = after(received, sent[-1], *others)
        sent.append(relay_step(tick, received, products, cotangent))
        if tick < ticks - LAG:
            moved.append(down(sent[-1]))

    near = [kv_rows] + [swap(kv_rows, relation) for relation in same[1 : 3 if chips == 4 else chips]]
    far = [swap(kv_rows, other_core)]
    columns = split_columns(inputs)
    left = lax.all_to_all(columns, "dp", 0, 0, tiled=True)
    products = list(weight_products([0], after(kv_rows, columns), weights))
    near = near[:1] + [after(piece, products[0]) for piece in near[1:]]
    products = [after(product, far[0], near[1]) for product in products]
    relay()
    products += weight_products([1], after(kv_rows, sent[0]), weights)
    relay()
    far.append(swap(near[1], other_core))
    for piece in near[2 : 2 if chips == 4 else chips]:
        far.append(swap(piece, other_core))
    if chips == 4:
        near.append(swap(near[1], same[2]))
    products += weight_products(list(range(LAG, CHUNKS)), after(kv_rows, sent[1]), weights)
    relay(products[-1])
    relay()
    if chips == 4:
        for piece in near[2:]:
            far.extend(swap(half, other_core) for half in cut(after(piece, sent[2]), 2))

    buffer, mine, theirs = gradient(
        left, same + crossed, near + far, after(moment, sent[3]), scale_grad, slots
    )
    relay(buffer)
    received = swap(after(theirs, sent[4]), other_core)
    relay(theirs)
    sums = add_pairs(after(mine, sent[5]), received)
    grams = [sums[0]] + [swap(sums[d], (CORES * d, CORES * d)) for d in range(1, chips)]
    relay(*grams[1:])
    mix = mixing([after(grams[0], sent[6])] + grams[1:], scale, slots)
    mixes = [mix] + [swap(mix, (CORES * d, CORES * d)) for d in range(1, chips)]
    relay(mix)
    far_mix = swap(after(mix, moved[6]), other_core)
    far_mixes = swap(join(mixes), other_core)
    update, outgoing = apply_mixing(after(buffer, sent[7]), mixes, far_mix, far_mixes, slots, sent)
    outgoing = last_step([after(m, update) for m in moved[-LAG:]], products[-LAG:], outgoing)
    return (update[None], outgoing[None])


def solution(mesh):
    in_specs = (
        P("pipe", "dp", None),
        P("dp", None),
        P("pipe", "dp", None),
        P("pipe", None, None),
        P("pipe", "dp", None),
    )
    out_specs = (P("pipe", "dp", None), P("pipe", "dp", None))
    return jax.shard_map(shards, mesh=mesh, in_specs=in_specs, out_specs=out_specs, check_vma=False)
```
